32 devices in a mesh: pb: 8 (over z, core), kv: 4 (over y, x).
Axes of the slice: x: 2, y: 2, z: 4, core: 2. Of those that a mesh axis runs over, the one named last changes fastest.
Arguments:
- queries: bfloat16 [49152, 1024], P(('pb', 'kv')), may hold values from -8 to 8
- keys: bfloat16 [65536, 128], P(('kv', 'pb')), may hold values from -6 to 6
- values: bfloat16 [65536, 128], P(('kv', 'pb')), may hold values from -6 to 6
- selected: int32 [768, 14], P(('pb', 'kv')), may hold values from 1 to 1022, as said below
Outputs:
- attended: bfloat16 [49152, 1024], P(('pb', 'kv'))
The draws below stay inside these ranges and needn't reach their ends.
Inputs may be any that keep to these rules, and one draw needn't show every extreme that they name: `selected`: each row names 14 different blocks, never block 0 or block 1023. Key device k holds blocks k * 32 to (k + 1) * 32 - 1, devices counted with kv slowest; query device d holds query blocks d * 24 to (d + 1) * 24 - 1, devices counted with pb slowest. The query blocks of one device name together at most 2 distinct blocks of one key device, and in every draw some key device has exactly 2 named by every query device.
All inputs are finite; a program needn't handle non-finite values.
Results may differ from the reference program's by a relative error of at most 0.0046.
Values may be sent and summed in bfloat16 or wider, within the bound.
No kernel may reach another device: no remote copies, remote signals or barrier semaphores. Data moves between devices by JAX's collectives and lax.ppermute only.
A program may use at most 128 MiB of HBM per device.

```python
import math
import jax
import jax.numpy as jnp
from jax import lax

H = 8
DH = 128
BLOCK = 64
TOPN = 16
QB = 64
TOKENS = 49152
CONTEXT = 65536
NQB = 768
QBLK_DEV = 24
BLK_DEV = 32
FREE = 14
DEVICES = 32


def draw_queries(key, part):
    own_key = jax.random.fold_in(key, 11)
    return jnp.clip(jax.random.normal(own_key, (TOKENS, H * DH), jnp.float32), -6.0, 6.0).astype(jnp.bfloat16)


def draw_keys(key, part):
    own_key = jax.random.fold_in(key, 13)
    return jnp.clip(jax.random.normal(own_key, (CONTEXT, DH), jnp.float32), -6.0, 6.0).astype(jnp.bfloat16)


def draw_selected(key, part):
    first_key, second_key, order_key, favor_key = jax.random.split(key, 4)
    owners = jnp.arange(DEVICES, dtype=jnp.int32)
    shift_up = (owners == 0).astype(jnp.int32)
    room = BLK_DEV - (owners == 0).astype(jnp.int32) - (owners == DEVICES - 1).astype(jnp.int32)
    first_pick = jax.random.randint(first_key, (DEVICES, DEVICES), 0, 2 ** 20) % room[None, :]
    stride = 1 + jax.random.randint(second_key, (DEVICES, DEVICES), 0, 2 ** 20) % (room[None, :] - 1)
    second_pick = (first_pick + stride) % room[None, :]
    local_ids = jnp.stack([first_pick, second_pick], axis=2) + shift_up[None, :, None]
    candidates = owners[None, :, None] * BLK_DEV + local_ids
    favored = jax.random.randint(favor_key, (), 0, DEVICES)
    order_scores = jax.random.randint(order_key, (DEVICES, DEVICES), 0, 2 ** 20) * DEVICES + owners[None, :]
    order_scores = order_scores + (owners[None, :] == favored).astype(jnp.int32) * 2 ** 29
    ranking = lax.top_k(order_scores, DEVICES)[1].astype(jnp.int32)
    half = FREE // 2
    blocks_all = jnp.arange(NQB, dtype=jnp.int32)
    device_of = blocks_all // QBLK_DEV
    place = ((blocks_all % QBLK_DEV)[:, None] * half + jnp.arange(half, dtype=jnp.int32)[None, :]) % DEVICES
    owner_pick = jnp.take_along_axis(ranking[device_of], place, axis=1)
    pairs = candidates[device_of[:, None], owner_pick]
    return pairs.reshape(NQB, FREE).astype(jnp.int32)


def level_of(stream_key, shape, pieces, low, largest):
    def one(axis_at, parts):
        heights = jax.random.uniform(jax.random.fold_in(jax.random.fold_in(stream_key, 6), axis_at), (parts,), jnp.float32, low / len(pieces), largest / len(pieces))
        return jnp.repeat(jnp.exp(heights), shape[axis_at] // parts).reshape((-1,) + (1,) * (len(shape) - axis_at - 1))

    factor_of = one(*pieces[0])
    for cut in pieces[1:]:
        factor_of = factor_of * one(*cut)
    return factor_of


def normal_values(key, extent, scale, bound, shards=(), kind=jnp.bfloat16):
    entries = jax.random.normal(key, extent, jnp.float32) * scale
    if len(shards) > 0:
        entries = level_of(key, extent, shards, -0.22, 0.18) * entries
    return jnp.clip(entries, min=-bound, max=bound).astype(kind)


def setup_inputs(seed: int = 0) -> dict:
    splits = jax.random.split(jax.random.key(seed), 5)
    queries = draw_queries(jax.random.fold_in(splits[4], 71), 0)
    keys = draw_keys(jax.random.fold_in(splits[4], 71), 0)
    values = normal_values(splits[2], (CONTEXT, DH), 1.0, 6.0, ((0, 32),))
    selected = draw_selected(jax.random.fold_in(splits[4], 71), 0)
    return {"queries": queries, "keys": keys, "values": values, "selected": selected}


def reference(queries, keys, values, selected):
    query_blocks = queries.shape[0] // QB
    block_total = keys.shape[0] // BLOCK
    forced = jnp.broadcast_to(jnp.array([0, block_total - 1], jnp.int32), (query_blocks, 2))
    lists = jnp.concatenate([forced, selected.astype(jnp.int32)], axis=1)
    group_size = math.gcd(query_blocks, 16)
    q_groups = queries.reshape(query_blocks // group_size, group_size, QB * H, DH)
    l_groups = lists.reshape(query_blocks // group_size, group_size, TOPN)
    key_blocks = keys.reshape(block_total, BLOCK, DH)
    value_blocks = values.reshape(block_total, BLOCK, DH)

    def attend(operands):
        q_block, block_ids = operands
        flat_ids = block_ids.reshape(-1)
        k_rows = jnp.take(key_blocks, flat_ids, axis=0).reshape(group_size, TOPN * BLOCK, DH).astype(jnp.float32)
        v_rows = jnp.take(value_blocks, flat_ids, axis=0).reshape(group_size, TOPN * BLOCK, DH).astype(jnp.float32)
        scores = jnp.einsum("gqd,gkd->gqk", q_block.astype(jnp.float32), k_rows) * (DH ** -0.5)
        weights = jnp.exp(scores - jnp.max(scores, axis=-1, keepdims=True))
        totals = jnp.sum(weights, axis=-1, keepdims=True)
        rounded = lax.optimization_barrier(weights.astype(jnp.bfloat16)).astype(jnp.float32)
        weighted = jnp.einsum("gqk,gkd->gqd", rounded, v_rows)
        return (weighted / totals).astype(jnp.bfloat16)

    result = lax.map(attend, (q_groups, l_groups))
    return result.reshape(query_blocks * QB, H * DH)
```

```python
import functools
import math

import jax
import jax.numpy as jnp
from jax import lax
from jax.experimental import pallas as pl
from jax.experimental.pallas import tpu as pltpu
from jax.sharding import Mesh
from jax.sharding import PartitionSpec as P

H = 8
DH = 128
BLOCK = 64
FREE = 14
QB = 64
CAP = 2
SCALE = DH ** -0.5 * math.log2(math.e)
HALF = ("pl", "kv")
ALL = ("hz", "pl", "kv")


def exchange(array, axes):
    return lax.all_to_all(array, axes, split_axis=0, concat_axis=0, tiled=True)


def attend(per_step, codes, q_ref, k_ref, near_ref, far_ref, forced_ref, out_ref):
    ones = jnp.ones((4 * BLOCK, DH), jnp.bfloat16)
    step = pl.program_id(0)
    for n in range(per_step):
        rows = q_ref[n * QB : (n + 1) * QB, :]
        stacked = jnp.concatenate([rows[:, h * DH : (h + 1) * DH] for h in range(H)], axis=0)
        key_tiles = [forced_ref[0, :BLOCK, :], forced_ref[1, :BLOCK, :]]
        value_tiles = [forced_ref[0, BLOCK:, :], forced_ref[1, BLOCK:, :]]
        for i in range(FREE):
            code = codes[(step * per_step + n) * FREE + i]
            source, slot = code // 4, code % 4
            key_tiles.append(k_ref[source, pl.ds(pl.multiple_of(slot * BLOCK, BLOCK), BLOCK), :])
            is_far = slot // 2
            second = slot % 2
            far = far_ref[source, second]
            near = near_ref[source, 2 + second]
            value_tiles.append(jnp.where(is_far == 1, far, near))
        key_groups = [jnp.concatenate(key_tiles[g * 4 : g * 4 + 4], axis=0) for g in range(4)]
        value_groups = [
            jnp.concatenate([jnp.concatenate(value_tiles[g * 4 : g * 4 + 4], axis=0), ones], axis=1)
            for g in range(4)
        ]
        for r in range(4):
            part = stacked[r * 128 : (r + 1) * 128]
            scores = [
                lax.dot_general(
                    part, k, (((1,), (1,)), ((), ())), preferred_element_type=jnp.float32
                )
                for k in key_groups
            ]
            top = functools.reduce(jnp.maximum, scores)
            top = jnp.max(top, axis=1, keepdims=True)
            total = None
            for s, v in zip(scores, value_groups):
                weights = jnp.exp2((s - top) * SCALE).astype(jnp.bfloat16)
                product = jnp.dot(weights, v, preferred_element_type=jnp.float32)
                total = product if total is None else total + product
            done = (total[:, :DH] / total[:, DH:]).astype(jnp.bfloat16)
            for i in range(2):
                h = r * 2 + i
                out_ref[n * QB : (n + 1) * QB, h * DH : (h + 1) * DH] = done[i * QB : (i + 1) * QB]


def per_device(queries, keys, values, selected):
    half_count = lax.axis_size("pl") * lax.axis_size("kv")
    kv_count = lax.axis_size("kv")
    pb_count = 2 * lax.axis_size("pl")
    devices = 2 * half_count
    blocks_here = keys.shape[0] // BLOCK
    query_blocks = queries.shape[0] // QB
    my_half = lax.axis_index("hz")
    me = lax.axis_index(ALL)
    swap = [(0, 1), (1, 0)]

    key_tiles = keys.reshape(blocks_here, BLOCK, DH)
    value_tiles = values.reshape(blocks_here, BLOCK, DH)
    far_keys = lax.ppermute(keys, "hz", swap).reshape(blocks_here, BLOCK, DH)

    flat = selected.reshape(-1)
    owner = flat // blocks_here
    local = flat % blocks_here
    place = owner % pb_count * kv_count + owner // pb_count
    second = jnp.any(
        (owner[:, None] == owner[None, :]) & (flat[None, :] < flat[:, None]), axis=1
    ).astype(jnp.int32)
    hit = place[None, :] == jnp.arange(devices, dtype=jnp.int32)[:, None]
    low = jnp.min(jnp.where(hit, local[None, :], blocks_here - 1), axis=1)
    high = jnp.max(jnp.where(hit, local[None, :], 0), axis=1)
    pairs = jnp.stack([low, high], axis=1).reshape(2, half_count, 2)
    wants = jnp.concatenate([pairs, pairs[::-1]], axis=2).reshape(devices, 4)
    codes = place % half_count * 4 + (place // half_count != my_half).astype(jnp.int32) * 2 + second

    piece = 2 * BLOCK // half_count
    edge = jnp.where(
        me == 0,
        jnp.concatenate([keys[:BLOCK], values[:BLOCK]], axis=0),
        jnp.concatenate([keys[-BLOCK:], values[-BLOCK:]], axis=0),
    ).reshape(half_count, piece, DH)
    header = jnp.pad(wants.astype(jnp.bfloat16)[:, None, :], ((0, 0), (0, 7), (0, DH - 4)))
    message = jnp.concatenate([header, jnp.concatenate([edge, edge], axis=0)], axis=1)
    answer = exchange(message, ALL)
    asked = answer[:, 0, :4].astype(jnp.int32).reshape(2, half_count, 4)
    asked_mine = jnp.where(my_half == 0, asked[0], asked[1])
    asked_other = jnp.where(my_half == 0, asked[1], asked[0])
    pieces = jnp.concatenate([answer[0, 8:], answer[devices - 1, 8:]], axis=0)

    wanted_values = jnp.concatenate([asked_other[:, :2], asked_mine[:, :2]], axis=1)
    value_parcel = jnp.take(value_tiles, wanted_values.reshape(-1), axis=0).reshape(
        half_count, 4, BLOCK, DH
    )
    near_values = exchange(value_parcel, HALF)
    far_values = lax.ppermute(near_values[:, :2], "hz", swap)

    near_keys = jnp.take(key_tiles, asked_mine[:, :2].reshape(-1), axis=0)
    passed_keys = jnp.take(far_keys, asked_mine[:, 2:].reshape(-1), axis=0)
    key_parcel = jnp.concatenate(
        [
            near_keys.reshape(half_count, 2 * BLOCK, DH),
            passed_keys.reshape(half_count, 2 * BLOCK, DH),
            jnp.broadcast_to(pieces[None], (half_count, 2 * piece, DH)),
        ],
        axis=1,
    )
    key_table = exchange(key_parcel, HALF)
    forced = (
        key_table[:, 4 * BLOCK :]
        .reshape(half_count, 2, piece, DH)
        .transpose(1, 0, 2, 3)
        .reshape(2, 2 * BLOCK, DH)
    )

    per_step = math.gcd(query_blocks, 4)
    whole = lambda shape: pl.BlockSpec(shape, lambda i, c: (0,) * len(shape))
    return pl.pallas_call(
        functools.partial(attend, per_step),
        out_shape=jax.ShapeDtypeStruct(queries.shape, queries.dtype),
        grid_spec=pltpu.PrefetchScalarGridSpec(
            num_scalar_prefetch=1,
            grid=(query_blocks // per_step,),
            in_specs=[
                pl.BlockSpec((per_step * QB, H * DH), lambda i, c: (i, 0)),
                whole(key_table.shape),
                whole(near_values.shape),
                whole(far_values.shape),
                whole(forced.shape),
            ],
            out_specs=pl.BlockSpec((per_step * QB, H * DH), lambda i, c: (i, 0)),
        ),
        compiler_params=pltpu.CompilerParams(vmem_limit_bytes=56 << 20),
    )(codes, queries, key_table, near_values, far_values, forced)


def solution(mesh):
    pb_count, kv_count = mesh.shape["pb"], mesh.shape["kv"]
    split = Mesh(mesh.devices.reshape(2, pb_count // 2, kv_count), ALL)
    by_query = P(("hz", "pl", "kv"), None)
    by_key = P(("kv", "hz", "pl"), None)
    return jax.shard_map(
        per_device,
        mesh=split,
        in_specs=(by_query, by_key, by_key, by_query),
        out_specs=by_query,
        check_vma=False,
    )
```

```python
import functools
import math

import jax
import jax.numpy as jnp
from jax import lax
from jax.experimental import pallas as pl
from jax.experimental.pallas import tpu as pltpu
from jax.sharding import PartitionSpec as P

H = 8
DH = 128
BLOCK = 64
FREE = 14
QB = 64
CAP = 2
HEADER = 8
SCALE = DH ** -0.5 * math.log2(math.e)
ALL = ("pb", "kv")


def exchange(array):
    return lax.all_to_all(array, ALL, split_axis=0, concat_axis=0, tiled=True)


def attend(per_step, codes, q_ref, table_ref, forced_ref, out_ref):
    ones = jnp.ones((4 * BLOCK, DH), jnp.bfloat16)
    step = pl.program_id(0)
    for n in range(per_step):
        rows = q_ref[n * QB : (n + 1) * QB, :]
        stacked = jnp.concatenate([rows[:, h * DH : (h + 1) * DH] for h in range(H)], axis=0)
        key_tiles = [forced_ref[0, :BLOCK, :], forced_ref[1, :BLOCK, :]]
        value_tiles = [forced_ref[0, BLOCK:, :], forced_ref[1, BLOCK:, :]]
        for i in range(FREE):
            code = codes[(step * per_step + n) * FREE + i]
            source = code // CAP
            row = pl.multiple_of(code % CAP * BLOCK, BLOCK)
            key_tiles.append(table_ref[source, pl.ds(row, BLOCK), :])
            value_tiles.append(table_ref[source, pl.ds(row + CAP * BLOCK, BLOCK), :])
        key_groups = [jnp.concatenate(key_tiles[g * 4 : g * 4 + 4], axis=0) for g in range(4)]
        value_groups = [
            jnp.concatenate([jnp.concatenate(value_tiles[g * 4 : g * 4 + 4], axis=0), ones], axis=1)
            for g in range(4)
        ]
        for r in range(4):
            part = stacked[r * 128 : (r + 1) * 128]
            scores = [
                lax.dot_general(
                    part, k, (((1,), (1,)), ((), ())), preferred_element_type=jnp.float32
                )
                for k in key_groups
            ]
            top = functools.reduce(jnp.maximum, scores)
            top = jnp.max(top, axis=1, keepdims=True)
            total = None
            for s, v in zip(scores, value_groups):
                weights = jnp.exp2((s - top) * SCALE).astype(jnp.bfloat16)
                product = jnp.dot(weights, v, preferred_element_type=jnp.float32)
                total = product if total is None else total + product
            done = (total[:, :DH] / total[:, DH:]).astype(jnp.bfloat16)
            for i in range(2):
                h = r * 2 + i
                out_ref[n * QB : (n + 1) * QB, h * DH : (h + 1) * DH] = done[i * QB : (i + 1) * QB]


def per_device(queries, keys, values, selected):
    pb_count = lax.axis_size("pb")
    kv_count = lax.axis_size("kv")
    devices = pb_count * kv_count
    blocks_here = keys.shape[0] // BLOCK
    query_blocks = queries.shape[0] // QB

    flat = selected.reshape(-1)
    owner = flat // blocks_here
    local = flat % blocks_here
    place = owner % pb_count * kv_count + owner // pb_count
    second = jnp.any(
        (owner[:, None] == owner[None, :]) & (flat[None, :] < flat[:, None]), axis=1
    ).astype(jnp.int32)
    codes = place * CAP + second
    hit = place[None, :] == jnp.arange(devices, dtype=jnp.int32)[:, None]
    low = jnp.min(jnp.where(hit, local[None, :], blocks_here - 1), axis=1)
    high = jnp.max(jnp.where(hit, local[None, :], 0), axis=1)
    wants = jnp.stack([low, high], axis=1).astype(jnp.bfloat16)

    span = 2 * BLOCK * DH // devices
    edges = jnp.stack(
        [
            jnp.concatenate([keys[:BLOCK], values[:BLOCK]], axis=0),
            jnp.concatenate([keys[-BLOCK:], values[-BLOCK:]], axis=0),
        ]
    ).reshape(2, devices, span)
    edges = edges.transpose(1, 0, 2).reshape(devices, 2 * span // DH, DH)
    header = jnp.pad(wants[:, None, :], ((0, 0), (0, HEADER - 1), (0, DH - CAP)))
    answer = exchange(jnp.concatenate([header, edges], axis=1))
    asked = answer[:, 0, :CAP].astype(jnp.int32)
    piece = jnp.concatenate(
        [answer[0, HEADER:].reshape(2, span)[:1], answer[devices - 1, HEADER:].reshape(2, span)[1:]]
    ).reshape(2 * span // DH, DH)

    def picked(array):
        tiles = jnp.take(array.reshape(blocks_here, BLOCK, DH), asked.reshape(-1), axis=0)
        return tiles.reshape(devices, CAP * BLOCK, DH)

    parcel = jnp.concatenate(
        [picked(keys), picked(values), jnp.broadcast_to(piece[None], (devices,) + piece.shape)],
        axis=1,
    )
    table = exchange(parcel)
    forced = (
        table[:, 2 * CAP * BLOCK :]
        .reshape(devices, 2, span)
        .transpose(1, 0, 2)
        .reshape(2, 2 * BLOCK, DH)
    )

    per_step = math.gcd(query_blocks, 4)
    whole = lambda shape: pl.BlockSpec(shape, lambda i, c: (0,) * len(shape))
    return pl.pallas_call(
        functools.partial(attend, per_step),
        out_shape=jax.ShapeDtypeStruct(queries.shape, queries.dtype),
        grid_spec=pltpu.PrefetchScalarGridSpec(
            num_scalar_prefetch=1,
            grid=(query_blocks // per_step,),
            in_specs=[
                pl.BlockSpec((per_step * QB, H * DH), lambda i, c: (i, 0)),
                whole(table.shape),
                whole(forced.shape),
            ],
            out_specs=pl.BlockSpec((per_step * QB, H * DH), lambda i, c: (i, 0)),
        ),
        compiler_params=pltpu.CompilerParams(vmem_limit_bytes=56 << 20),
    )(codes, queries, table, forced)


def solution(mesh):
    by_query = P(("pb", "kv"), None)
    by_key = P(("kv", "pb"), None)
    return jax.shard_map(
        per_device,
        mesh=mesh,
        in_specs=(by_query, by_key, by_key, by_query),
        out_specs=by_query,
        check_vma=False,
    )
```

```python
import functools
import math

import jax
import jax.numpy as jnp
from jax import lax
from jax.experimental import pallas as pl
from jax.experimental.pallas import tpu as pltpu
from jax.sharding import PartitionSpec as P

H = 8
DH = 128
BLOCK = 64
FREE = 14
QB = 64
CAP = 2
PIECES = 32
PIECE = 4 * BLOCK // PIECES
CHUNK = 256
GROUP = 4
SCALE = DH ** -0.5 * math.log2(math.e)
ALL = ("pb", "kv")


def exchange(array):
    return lax.all_to_all(array, ALL, split_axis=0, concat_axis=0, tiled=True)


def prepare(devices, blocks_here, place_ref, local_ref, fk, fv, lk, lv, code_ref, message_ref):
    rows, columns = place_ref.shape
    ids = lax.broadcasted_iota(jnp.int32, (devices, columns), 0)
    low = jnp.full((devices, columns), blocks_here - 1, jnp.int32)
    high = jnp.zeros((devices, columns), jnp.int32)
    for r in range(rows):
        hit = place_ref[r : r + 1, :] == ids
        local = jnp.broadcast_to(local_ref[r : r + 1, :], ids.shape)
        low = jnp.where(hit, jnp.minimum(low, local), low)
        high = jnp.where(hit, jnp.maximum(high, local), high)
    low = jnp.min(low, axis=1, keepdims=True)
    high = jnp.max(high, axis=1, keepdims=True)
    for r in range(rows):
        place, local = place_ref[r : r + 1, :], local_ref[r : r + 1, :]
        above = jnp.where((place == ids) & (local > low), 1, 0)
        code_ref[r : r + 1, :] = place * CAP + jnp.max(above, axis=0, keepdims=True)
    lane = lax.broadcasted_iota(jnp.int32, (devices, DH), 1)
    wants = jnp.where(lane == 0, low, jnp.where(lane == 1, high, 0)).astype(jnp.float32)
    wants = jnp.broadcast_to(wants[:, None, :], (devices, PIECE, DH))
    message_ref[:, :PIECE, :] = wants.astype(jnp.bfloat16)
    edges = jnp.concatenate([fk[...], fv[...], lk[...], lv[...]], axis=0).astype(jnp.float32)
    edges = edges.reshape(PIECES, PIECE, DH).astype(jnp.bfloat16)
    for at in range(0, devices, PIECES):
        message_ref[at : at + PIECES, PIECE:, :] = edges


def pack(devices, asked, answer_ref, k_ref, v_ref, parcel_ref):
    late = asked[devices * CAP]
    piece = answer_ref[late * (devices - 1), PIECE:, :]

    @pl.loop(0, devices)
    def _(m):
        for slot in range(CAP):
            row = pl.multiple_of(asked[m * CAP + slot] * BLOCK, BLOCK)
            at = slot * BLOCK
            parcel_ref[m, at : at + BLOCK, :] = k_ref[pl.ds(row, BLOCK), :]
            at += CAP * BLOCK
            parcel_ref[m, at : at + BLOCK, :] = v_ref[pl.ds(row, BLOCK), :]
        parcel_ref[m, 2 * CAP * BLOCK :, :] = piece


def attend(per_step, codes, q_ref, table_ref, out_ref, edge_ref):
    step = pl.program_id(0)

    @pl.when(step == 0)
    def _():
        edges = table_ref[:PIECES, 2 * CAP * BLOCK :, :].astype(jnp.float32)
        edge_ref[...] = edges.reshape(4 * BLOCK, DH).astype(jnp.bfloat16)

    ones = jnp.ones((GROUP * BLOCK, DH), jnp.bfloat16)
    groups = (FREE + 2) // GROUP
    chunks = QB * H // CHUNK

    def load(n):
        rows = q_ref[n * QB : (n + 1) * QB, :]
        stacked = jnp.concatenate([rows[:, h * DH : (h + 1) * DH] for h in range(H)], axis=0)
        key_tiles = [edge_ref[:BLOCK, :], edge_ref[2 * BLOCK : 3 * BLOCK, :]]
        value_tiles = [edge_ref[BLOCK : 2 * BLOCK, :], edge_ref[3 * BLOCK :, :]]
        for i in range(FREE):
            code = codes[step * per_step + n, i]
            source = code // CAP
            row = pl.multiple_of(code % CAP * BLOCK, BLOCK)
            key_tiles.append(table_ref[source, pl.ds(row, BLOCK), :])
            value_tiles.append(table_ref[source, pl.ds(row + CAP * BLOCK, BLOCK), :])
        join = lambda tiles, g: jnp.concatenate(tiles[g * GROUP : (g + 1) * GROUP], axis=0)
        return (
            stacked,
            [join(key_tiles, g) for g in range(groups)],
            [jnp.concatenate([join(value_tiles, g), ones], axis=1) for g in range(groups)],
        )

    def score(block, c):
        part = block[0][c * CHUNK : (c + 1) * CHUNK]
        scores = [
            lax.dot_general(part, k, (((1,), (1,)), ((), ())), preferred_element_type=jnp.float32)
            for k in block[1]
        ]
        tops = [jnp.max(s, axis=1, keepdims=True) for s in scores]
        return scores, functools.reduce(jnp.maximum, tops)

    def finish(block, n, c, scores, top):
        total = None
        for s, v in zip(scores, block[2]):
            weights = jnp.exp2((s - top) * SCALE).astype(jnp.bfloat16)
            product = jnp.dot(weights, v, preferred_element_type=jnp.float32)
            total = product if total is None else total + product
        done = (total[:, :DH] / total[:, DH:]).astype(jnp.bfloat16)
        for i in range(CHUNK // QB):
            h = c * (CHUNK // QB) + i
            out_ref[n * QB : (n + 1) * QB, h * DH : (h + 1) * DH] = done[i * QB : (i + 1) * QB]

    waiting = None
    for n in range(per_step):
        block = load(n)
        for c in range(chunks):
            scored = (block, n, c, *score(block, c))
            if waiting is not None:
                finish(*waiting)
            waiting = scored
    finish(*waiting)


def per_device(queries, keys, values, selected):
    pb_count = lax.axis_size("pb")
    kv_count = lax.axis_size("kv")
    devices = pb_count * kv_count
    blocks_here = keys.shape[0] // BLOCK
    query_blocks = queries.shape[0] // QB

    owner = selected // blocks_here
    local = selected % blocks_here
    place = owner % pb_count * kv_count + owner // pb_count
    first = pl.BlockSpec((BLOCK, DH), lambda i: (0, 0))
    last = pl.BlockSpec((BLOCK, DH), lambda i: (blocks_here - 1, 0))
    held = pl.BlockSpec(selected.shape, lambda i: (0, 0))
    message_shape = (devices, 2 * PIECE, DH)
    codes, message = pl.pallas_call(
        functools.partial(prepare, devices, blocks_here),
        grid=(1,),
        in_specs=[held, held, first, first, last, last],
        out_specs=[held, pl.BlockSpec(message_shape, lambda i: (0, 0, 0))],
        out_shape=[
            jax.ShapeDtypeStruct(selected.shape, jnp.int32),
            jax.ShapeDtypeStruct(message_shape, jnp.bfloat16),
        ],
    )(place, local, keys, values, keys, values)

    answer = exchange(message)
    late = (lax.axis_index(ALL) % PIECES >= PIECES // 2).astype(jnp.int32)
    asked = jnp.concatenate([answer[:, 0, :CAP].astype(jnp.int32).reshape(-1), late[None]])
    parcel_shape = (devices, 2 * CAP * BLOCK + PIECE, DH)
    parcel_bytes = 2 * math.prod(parcel_shape)
    parcel = pl.pallas_call(
        functools.partial(pack, devices),
        grid_spec=pltpu.PrefetchScalarGridSpec(
            num_scalar_prefetch=1,
            grid=(),
            in_specs=[pl.BlockSpec(memory_space=pltpu.VMEM)] * 3,
            out_specs=pl.BlockSpec(memory_space=pltpu.VMEM),
        ),
        out_shape=jax.ShapeDtypeStruct(parcel_shape, keys.dtype),
        compiler_params=pltpu.CompilerParams(vmem_limit_bytes=(8 << 20) + parcel_bytes),
    )(asked, answer, keys, values)
    table = exchange(parcel)

    per_step = math.gcd(query_blocks, 6)
    return pl.pallas_call(
        functools.partial(attend, per_step),
        out_shape=jax.ShapeDtypeStruct(queries.shape, queries.dtype),
        grid_spec=pltpu.PrefetchScalarGridSpec(
            num_scalar_prefetch=1,
            grid=(query_blocks // per_step,),
            in_specs=[
                pl.BlockSpec((per_step * QB, H * DH), lambda i, c: (i, 0)),
                pl.BlockSpec(parcel_shape, lambda i, c: (0, 0, 0)),
            ],
            out_specs=pl.BlockSpec((per_step * QB, H * DH), lambda i, c: (i, 0)),
            scratch_shapes=[pltpu.VMEM((4 * BLOCK, DH), jnp.bfloat16)],
        ),
        compiler_params=pltpu.CompilerParams(vmem_limit_bytes=56 << 20),
    )(codes, queries, table)


def solution(mesh):
    by_query = P(("pb", "kv"), None)
    by_key = P(("kv", "pb"), None)
    return jax.shard_map(
        per_device,
        mesh=mesh,
        in_specs=(by_query, by_key, by_key, by_query),
        out_specs=by_query,
        check_vma=False,
    )
```

```python
import functools
import math

import jax
import jax.numpy as jnp
from jax import lax
from jax.experimental import pallas as pl
from jax.experimental.pallas import tpu as pltpu
from jax.sharding import PartitionSpec as P

H = 8
DH = 128
BLOCK = 64
FREE = 14
QB = 64
CAP = 2
PIECES = 32
PIECE = 4 * BLOCK // PIECES
CHUNK = 256
GROUP = 4
SCALE = DH ** -0.5 * math.log2(math.e)
ALL = ("pb", "kv")


def exchange(array):
    return lax.all_to_all(array, ALL, split_axis=0, concat_axis=0, tiled=True)


def divide(array, n):
    if n & (n - 1) == 0:
        return array >> (n.bit_length() - 1), array & (n - 1)
    return array // n, array % n


def prepare(pb_count, kv_count, blocks_here, selected_ref, fk, fv, lk, lv, code_ref, message_ref):
    devices = pb_count * kv_count
    rows, columns = selected_ref.shape
    owner, locals_ = divide(selected_ref[...], blocks_here)
    owner_kv, owner_pb = divide(owner, pb_count)
    places = owner_pb * kv_count + owner_kv
    ids = lax.broadcasted_iota(jnp.int32, (devices, columns), 0)
    low = jnp.full((devices, columns), blocks_here - 1, jnp.int32)
    high = jnp.zeros((devices, columns), jnp.int32)
    for r in range(rows):
        hit = places[r : r + 1, :] == ids
        local = jnp.broadcast_to(locals_[r : r + 1, :], ids.shape)
        low = jnp.where(hit, jnp.minimum(low, local), low)
        high = jnp.where(hit, jnp.maximum(high, local), high)
    low = jnp.min(low, axis=1, keepdims=True)
    high = jnp.max(high, axis=1, keepdims=True)
    for r in range(rows):
        place, local = places[r : r + 1, :], locals_[r : r + 1, :]
        above = jnp.where((place == ids) & (local > low), 1, 0)
        code_ref[r : r + 1, :] = place * CAP + jnp.max(above, axis=0, keepdims=True)
    lane = lax.broadcasted_iota(jnp.int32, (devices, DH), 1)
    wants = jnp.where(lane == 0, low, jnp.where(lane == 1, high, 0)).astype(jnp.float32)
    wants = jnp.broadcast_to(wants[:, None, :], (devices, PIECE, DH))
    message_ref[:, :PIECE, :] = wants.astype(jnp.bfloat16)
    edges = jnp.concatenate([fk[...], fv[...], lk[...], lv[...]], axis=0).astype(jnp.float32)
    edges = edges.reshape(PIECES, PIECE, DH).astype(jnp.bfloat16)
    for at in range(0, devices, PIECES):
        message_ref[at : at + PIECES, PIECE:, :] = edges


def pack(devices, asked, answer_ref, k_ref, v_ref, parcel_ref):
    late = asked[devices * CAP]
    piece = answer_ref[late * (devices - 1), PIECE:, :]

    @pl.loop(0, devices)
    def _(m):
        for slot in range(CAP):
            row = pl.multiple_of(asked[m * CAP + slot] * BLOCK, BLOCK)
            at = slot * BLOCK
            parcel_ref[m, at : at + BLOCK, :] = k_ref[pl.ds(row, BLOCK), :]
            at += CAP * BLOCK
            parcel_ref[m, at : at + BLOCK, :] = v_ref[pl.ds(row, BLOCK), :]
        parcel_ref[m, 2 * CAP * BLOCK :, :] = piece


def attend(per_step, codes, q_ref, table_ref, out_ref, edge_ref):
    step = pl.program_id(0)

    @pl.when(step == 0)
    def _():
        edges = table_ref[:PIECES, 2 * CAP * BLOCK :, :].astype(jnp.float32)
        edge_ref[...] = edges.reshape(4 * BLOCK, DH).astype(jnp.bfloat16)

    ones = jnp.ones((GROUP * BLOCK, DH), jnp.bfloat16)
    groups = (FREE + 2) // GROUP
    chunks = QB * H // CHUNK

    def load(n):
        rows = q_ref[n * QB : (n + 1) * QB, :]
        stacked = jnp.concatenate([rows[:, h * DH : (h + 1) * DH] for h in range(H)], axis=0)
        key_tiles = [edge_ref[:BLOCK, :], edge_ref[2 * BLOCK : 3 * BLOCK, :]]
        value_tiles = [edge_ref[BLOCK : 2 * BLOCK, :], edge_ref[3 * BLOCK :, :]]
        for i in range(FREE):
            code = codes[i, step * per_step + n]
            source = code // CAP
            row = pl.multiple_of(code % CAP * BLOCK, BLOCK)
            key_tiles.append(table_ref[source, pl.ds(row, BLOCK), :])
            value_tiles.append(table_ref[source, pl.ds(row + CAP * BLOCK, BLOCK), :])
        join = lambda tiles, g: jnp.concatenate(tiles[g * GROUP : (g + 1) * GROUP], axis=0)
        return (
            stacked,
            [join(key_tiles, g) for g in range(groups)],
            [jnp.concatenate([join(value_tiles, g), ones], axis=1) for g in range(groups)],
        )

    def score(block, c):
        part = block[0][c * CHUNK : (c + 1) * CHUNK]
        scores = [
            lax.dot_general(part, k, (((1,), (1,)), ((), ())), preferred_element_type=jnp.float32)
            for k in block[1]
        ]
        tops = [jnp.max(s, axis=1, keepdims=True) for s in scores]
        return scores, functools.reduce(jnp.maximum, tops)

    def finish(block, n, c, scores, top):
        total = None
        for s, v in zip(scores, block[2]):
            weights = jnp.exp2((s - top) * SCALE).astype(jnp.bfloat16)
            product = jnp.dot(weights, v, preferred_element_type=jnp.float32)
            total = product if total is None else total + product
        done = (total[:, :DH] / total[:, DH:]).astype(jnp.bfloat16)
        for i in range(CHUNK // QB):
            h = c * (CHUNK // QB) + i
            out_ref[n * QB : (n + 1) * QB, h * DH : (h + 1) * DH] = done[i * QB : (i + 1) * QB]

    waiting = None
    for n in range(per_step):
        block = load(n)
        for c in range(chunks):
            scored = (block, n, c, *score(block, c))
            if waiting is not None:
                finish(*waiting)
            waiting = scored
    finish(*waiting)


def per_device(queries, keys, values, selected):
    pb_count = lax.axis_size("pb")
    kv_count = lax.axis_size("kv")
    devices = pb_count * kv_count
    blocks_here = keys.shape[0] // BLOCK
    query_blocks = queries.shape[0] // QB

    listed = selected.T
    first = pl.BlockSpec((BLOCK, DH), lambda i: (0, 0))
    last = pl.BlockSpec((BLOCK, DH), lambda i: (blocks_here - 1, 0))
    held = pl.BlockSpec(listed.shape, lambda i: (0, 0))
    message_shape = (devices, 2 * PIECE, DH)
    codes, message = pl.pallas_call(
        functools.partial(prepare, pb_count, kv_count, blocks_here),
        grid=(1,),
        in_specs=[held, first, first, last, last],
        out_specs=[held, pl.BlockSpec(message_shape, lambda i: (0, 0, 0))],
        out_shape=[
            jax.ShapeDtypeStruct(listed.shape, jnp.int32),
            jax.ShapeDtypeStruct(message_shape, jnp.bfloat16),
        ],
    )(listed, keys, values, keys, values)

    answer = exchange(message)
    late = (lax.axis_index(ALL) % PIECES >= PIECES // 2).astype(jnp.int32)
    asked = jnp.concatenate([answer[:, 0, :CAP].astype(jnp.int32).reshape(-1), late[None]])
    parcel_shape = (devices, 2 * CAP * BLOCK + PIECE, DH)
    parcel_bytes = 2 * math.prod(parcel_shape)
    parcel = pl.pallas_call(
        functools.partial(pack, devices),
        grid_spec=pltpu.PrefetchScalarGridSpec(
            num_scalar_prefetch=1,
            grid=(1,),
            in_specs=[
                pl.BlockSpec(memory_space=pltpu.VMEM),
                pl.BlockSpec(keys.shape, lambda i, c: (0, 0)),
                pl.BlockSpec(values.shape, lambda i, c: (0, 0)),
            ],
            out_specs=pl.BlockSpec(memory_space=pltpu.VMEM),
        ),
        out_shape=jax.ShapeDtypeStruct(parcel_shape, keys.dtype),
        compiler_params=pltpu.CompilerParams(vmem_limit_bytes=(8 << 20) + parcel_bytes),
    )(asked, answer, keys, values)
    table = exchange(parcel)

    per_step = math.gcd(query_blocks, 6)
    return pl.pallas_call(
        functools.partial(attend, per_step),
        out_shape=jax.ShapeDtypeStruct(queries.shape, queries.dtype),
        grid_spec=pltpu.PrefetchScalarGridSpec(
            num_scalar_prefetch=1,
            grid=(query_blocks // per_step,),
            in_specs=[
                pl.BlockSpec((per_step * QB, H * DH), lambda i, c: (i, 0)),
                pl.BlockSpec(memory_space=pltpu.VMEM),
            ],
            out_specs=pl.BlockSpec((per_step * QB, H * DH), lambda i, c: (i, 0)),
            scratch_shapes=[pltpu.VMEM((4 * BLOCK, DH), jnp.bfloat16)],
        ),
        compiler_params=pltpu.CompilerParams(vmem_limit_bytes=(24 << 20) + parcel_bytes),
    )(codes, queries, table)


def solution(mesh):
    by_query = P(("pb", "kv"), None)
    by_key = P(("kv", "pb"), None)
    return jax.shard_map(
        per_device,
        mesh=mesh,
        in_specs=(by_query, by_key, by_key, by_query),
        out_specs=by_query,
        check_vma=False,
    )
```

```python
import functools
import math

import jax
import jax.numpy as jnp
from jax import lax
from jax.experimental import pallas as pl
from jax.experimental.pallas import tpu as pltpu
from jax.sharding import PartitionSpec as P

H = 8
DH = 128
BLOCK = 64
FREE = 14
QB = 64
CAP = 2
PIECES = 32
PIECE = 4 * BLOCK // PIECES
CHUNK = 256
GROUP = 4
SCALE = DH ** -0.5 * math.log2(math.e)
ALL = ("pb", "kv")


def exchange(array):
    return lax.all_to_all(array, ALL, split_axis=0, concat_axis=0, tiled=True)


def divide(array, n):
    if n & (n - 1) == 0:
        return array >> (n.bit_length() - 1), array & (n - 1)
    return array // n, array % n


def prepare(pb_count, kv_count, blocks_here, selected_ref, fk, fv, lk, lv, code_ref, message_ref):
    devices = pb_count * kv_count
    rows, columns = selected_ref.shape
    owner, locals_ = divide(selected_ref[...], blocks_here)
    owner_kv, owner_pb = divide(owner, pb_count)
    places = owner_pb * kv_count + owner_kv
    ids = lax.broadcasted_iota(jnp.int32, (devices, columns), 0)
    low = jnp.full((devices, columns), blocks_here - 1, jnp.int32)
    high = jnp.zeros((devices, columns), jnp.int32)
    for r in range(rows):
        hit = places[r : r + 1, :] == ids
        local = jnp.broadcast_to(locals_[r : r + 1, :], ids.shape)
        low = jnp.where(hit, jnp.minimum(low, local), low)
        high = jnp.where(hit, jnp.maximum(high, local), high)
    low = jnp.min(low, axis=1, keepdims=True)
    high = jnp.max(high, axis=1, keepdims=True)
    for r in range(rows):
        place, local = places[r : r + 1, :], locals_[r : r + 1, :]
        above = jnp.where((place == ids) & (local > low), 1, 0)
        code_ref[r : r + 1, :] = place * CAP + jnp.max(above, axis=0, keepdims=True)
    lane = lax.broadcasted_iota(jnp.int32, (devices, DH), 1)
    wants = jnp.where(lane == 0, low, jnp.where(lane == 1, high, 0)).astype(jnp.float32)
    wants = jnp.broadcast_to(wants[:, None, :], (devices, PIECE, DH))
    message_ref[:, :PIECE, :] = wants.astype(jnp.bfloat16)
    edges = jnp.concatenate([fk[...], fv[...], lk[...], lv[...]], axis=0).astype(jnp.float32)
    edges = edges.reshape(PIECES, PIECE, DH).astype(jnp.bfloat16)
    for at in range(0, devices, PIECES):
        message_ref[at : at + PIECES, PIECE:, :] = edges


def stage(k_ref, v_ref, held_ref):
    held_ref[0] = k_ref[...]
    held_ref[1] = v_ref[...]


def pack(devices, asked, answer_ref, held_ref, parcel_ref):
    late = asked[devices * CAP]
    piece = answer_ref[late * (devices - 1), PIECE:, :]

    @pl.loop(0, devices)
    def _(m):
        for slot in range(CAP):
            row = pl.multiple_of(asked[m * CAP + slot] * BLOCK, BLOCK)
            at = slot * BLOCK
            parcel_ref[m, at : at + BLOCK, :] = held_ref[0, pl.ds(row, BLOCK), :]
            at += CAP * BLOCK
            parcel_ref[m, at : at + BLOCK, :] = held_ref[1, pl.ds(row, BLOCK), :]
        parcel_ref[m, 2 * CAP * BLOCK :, :] = piece


def attend(per_step, codes, q_ref, table_ref, out_ref, edge_ref):
    step = pl.program_id(0)

    @pl.when(step == 0)
    def _():
        edges = table_ref[:PIECES, 2 * CAP * BLOCK :, :].astype(jnp.float32)
        edge_ref[...] = edges.reshape(4 * BLOCK, DH).astype(jnp.bfloat16)

    ones = jnp.ones((GROUP * BLOCK, DH), jnp.bfloat16)
    groups = (FREE + 2) // GROUP
    chunks = QB * H // CHUNK

    def load(n):
        rows = q_ref[n * QB : (n + 1) * QB, :]
        stacked = jnp.concatenate([rows[:, h * DH : (h + 1) * DH] for h in range(H)], axis=0)
        key_tiles = [edge_ref[:BLOCK, :], edge_ref[2 * BLOCK : 3 * BLOCK, :]]
        value_tiles = [edge_ref[BLOCK : 2 * BLOCK, :], edge_ref[3 * BLOCK :, :]]
        for i in range(FREE):
            code = codes[i, step * per_step + n]
            source = code // CAP
            row = pl.multiple_of(code % CAP * BLOCK, BLOCK)
            key_tiles.append(table_ref[source, pl.ds(row, BLOCK), :])
            value_tiles.append(table_ref[source, pl.ds(row + CAP * BLOCK, BLOCK), :])
        join = lambda tiles, g: jnp.concatenate(tiles[g * GROUP : (g + 1) * GROUP], axis=0)
        return (
            stacked,
            [join(key_tiles, g) for g in range(groups)],
            [jnp.concatenate([join(value_tiles, g), ones], axis=1) for g in range(groups)],
        )

    def score(block, c):
        part = block[0][c * CHUNK : (c + 1) * CHUNK]
        scores = [
            lax.dot_general(part, k, (((1,), (1,)), ((), ())), preferred_element_type=jnp.float32)
            for k in block[1]
        ]
        tops = [jnp.max(s, axis=1, keepdims=True) for s in scores]
        return scores, functools.reduce(jnp.maximum, tops)

    def finish(block, n, c, scores, top):
        total = None
        for s, v in zip(scores, block[2]):
            weights = jnp.exp2((s - top) * SCALE).astype(jnp.bfloat16)
            product = jnp.dot(weights, v, preferred_element_type=jnp.float32)
            total = product if total is None else total + product
        done = (total[:, :DH] / total[:, DH:]).astype(jnp.bfloat16)
        for i in range(CHUNK // QB):
            h = c * (CHUNK // QB) + i
            out_ref[n * QB : (n + 1) * QB, h * DH : (h + 1) * DH] = done[i * QB : (i + 1) * QB]

    waiting = None
    for n in range(per_step):
        block = load(n)
        for c in range(chunks):
            scored = (block, n, c, *score(block, c))
            if waiting is not None:
                finish(*waiting)
            waiting = scored
    finish(*waiting)


def per_device(queries, keys, values, selected):
    pb_count = lax.axis_size("pb")
    kv_count = lax.axis_size("kv")
    devices = pb_count * kv_count
    blocks_here = keys.shape[0] // BLOCK
    query_blocks = queries.shape[0] // QB

    listed = selected.T
    first = pl.BlockSpec((BLOCK, DH), lambda i: (0, 0))
    last = pl.BlockSpec((BLOCK, DH), lambda i: (blocks_here - 1, 0))
    held = pl.BlockSpec(listed.shape, lambda i: (0, 0))
    message_shape = (devices, 2 * PIECE, DH)
    codes, message = pl.pallas_call(
        functools.partial(prepare, pb_count, kv_count, blocks_here),
        grid=(1,),
        in_specs=[held, first, first, last, last],
        out_specs=[held, pl.BlockSpec(message_shape, lambda i: (0, 0, 0))],
        out_shape=[
            jax.ShapeDtypeStruct(listed.shape, jnp.int32),
            jax.ShapeDtypeStruct(message_shape, jnp.bfloat16),
        ],
    )(listed, keys, values, keys, values)

    held_tiles = pl.pallas_call(
        stage,
        grid=(1,),
        in_specs=[
            pl.BlockSpec(keys.shape, lambda i: (0, 0)),
            pl.BlockSpec(values.shape, lambda i: (0, 0)),
        ],
        out_specs=pl.BlockSpec(memory_space=pltpu.VMEM),
        out_shape=jax.ShapeDtypeStruct((2,) + keys.shape, keys.dtype),
        compiler_params=pltpu.CompilerParams(vmem_limit_bytes=8 << 20),
    )(keys, values)
    answer = exchange(message)
    late = (lax.axis_index(ALL) % PIECES >= PIECES // 2).astype(jnp.int32)
    asked = jnp.concatenate([answer[:, 0, :CAP].astype(jnp.int32).reshape(-1), late[None]])
    parcel_shape = (devices, 2 * CAP * BLOCK + PIECE, DH)
    parcel_bytes = 2 * math.prod(parcel_shape)
    parcel = pl.pallas_call(
        functools.partial(pack, devices),
        grid_spec=pltpu.PrefetchScalarGridSpec(
            num_scalar_prefetch=1,
            grid=(1,),
            in_specs=[pl.BlockSpec(memory_space=pltpu.VMEM)] * 2,
            out_specs=pl.BlockSpec(memory_space=pltpu.VMEM),
        ),
        out_shape=jax.ShapeDtypeStruct(parcel_shape, keys.dtype),
        compiler_params=pltpu.CompilerParams(vmem_limit_bytes=(8 << 20) + parcel_bytes),
    )(asked, answer, held_tiles)
    table = exchange(parcel)

    per_step = math.gcd(query_blocks, 12)
    return pl.pallas_call(
        functools.partial(attend, per_step),
        out_shape=jax.ShapeDtypeStruct(queries.shape, queries.dtype),
        grid_spec=pltpu.PrefetchScalarGridSpec(
            num_scalar_prefetch=1,
            grid=(query_blocks // per_step,),
            in_specs=[
                pl.BlockSpec((per_step * QB, H * DH), lambda i, c: (i, 0)),
                pl.BlockSpec(memory_space=pltpu.VMEM),
            ],
            out_specs=pl.BlockSpec((per_step * QB, H * DH), lambda i, c: (i, 0)),
            scratch_shapes=[pltpu.VMEM((4 * BLOCK, DH), jnp.bfloat16)],
        ),
        compiler_params=pltpu.CompilerParams(vmem_limit_bytes=(24 << 20) + parcel_bytes),
    )(codes, queries, table)


def solution(mesh):
    by_query = P(("pb", "kv"), None)
    by_key = P(("kv", "pb"), None)
    return jax.shard_map(
        per_device,
        mesh=mesh,
        in_specs=(by_query, by_key, by_key, by_query),
        out_specs=by_query,
        check_vma=False,
    )
```

```python
import functools
import math

import jax
import jax.numpy as jnp
from jax import lax
from jax.experimental import pallas as pl
from jax.experimental.pallas import tpu as pltpu
from jax.sharding import PartitionSpec as P

H = 8
DH = 128
BLOCK = 64
FREE = 14
QB = 64
CAP = 2
PIECES = 32
PIECE = 4 * BLOCK // PIECES
CHUNK = 256
GROUP = 4
TRUSTED = 2.0 ** 100
SCALE = DH ** -0.5 * math.log2(math.e)
ALL = ("pb", "kv")


def exchange(array):
    return lax.all_to_all(array, ALL, split_axis=0, concat_axis=0, tiled=True)


def divide(array, n):
    if n & (n - 1) == 0:
        return array >> (n.bit_length() - 1), array & (n - 1)
    return array // n, array % n


def prepare(pb_count, kv_count, blocks_here, selected_ref, fk, fv, lk, lv, code_ref, message_ref):
    devices = pb_count * kv_count
    rows, columns = selected_ref.shape
    owner, locals_ = divide(selected_ref[...], blocks_here)
    owner_kv, owner_pb = divide(owner, pb_count)
    places = owner_pb * kv_count + owner_kv
    ids = lax.broadcasted_iota(jnp.int32, (devices, columns), 0)
    low = jnp.full((devices, columns), blocks_here - 1, jnp.int32)
    high = jnp.zeros((devices, columns), jnp.int32)
    for r in range(rows):
        hit = places[r : r + 1, :] == ids
        local = jnp.broadcast_to(locals_[r : r + 1, :], ids.shape)
        low = jnp.where(hit, jnp.minimum(low, local), low)
        high = jnp.where(hit, jnp.maximum(high, local), high)
    low = jnp.min(low, axis=1, keepdims=True)
    high = jnp.max(high, axis=1, keepdims=True)
    for r in range(rows):
        place, local = places[r : r + 1, :], locals_[r : r + 1, :]
        above = jnp.where((place == ids) & (local > low), 1, 0)
        code_ref[r : r + 1, :] = place * CAP + jnp.max(above, axis=0, keepdims=True)
    lane = lax.broadcasted_iota(jnp.int32, (devices, DH), 1)
    wants = jnp.where(lane == 0, low, jnp.where(lane == 1, high, 0)).astype(jnp.float32)
    wants = jnp.broadcast_to(wants[:, None, :], (devices, PIECE, DH))
    message_ref[:, :PIECE, :] = wants.astype(jnp.bfloat16)
    edges = jnp.concatenate([fk[...], fv[...], lk[...], lv[...]], axis=0).astype(jnp.float32)
    edges = edges.reshape(PIECES, PIECE, DH).astype(jnp.bfloat16)
    for at in range(0, devices, PIECES):
        message_ref[at : at + PIECES, PIECE:, :] = edges


def stage(k_ref, v_ref, held_ref):
    held_ref[0] = k_ref[...]
    held_ref[1] = v_ref[...]


def pack(devices, asked, late, answer_ref, held_ref, parcel_ref):
    piece = answer_ref[late[0] * (devices - 1), PIECE:, :]

    @pl.loop(0, devices)
    def _(m):
        for slot in range(CAP):
            row = pl.multiple_of(asked[m * CAP + slot] * BLOCK, BLOCK)
            at = slot * BLOCK
            parcel_ref[m, at : at + BLOCK, :] = held_ref[0, pl.ds(row, BLOCK), :]
            at += CAP * BLOCK
            parcel_ref[m, at : at + BLOCK, :] = held_ref[1, pl.ds(row, BLOCK), :]
        parcel_ref[m, 2 * CAP * BLOCK :, :] = piece


def attend(per_step, codes, q_ref, table_ref, out_ref, edge_ref):
    step = pl.program_id(0)

    @pl.when(step == 0)
    def _():
        edges = table_ref[:PIECES, 2 * CAP * BLOCK :, :].astype(jnp.float32)
        edge_ref[...] = edges.reshape(4 * BLOCK, DH).astype(jnp.bfloat16)

    ones = jnp.ones((GROUP * BLOCK, DH), jnp.bfloat16)
    groups = (FREE + 2) // GROUP
    chunks = QB * H // CHUNK

    def load(n):
        rows = q_ref[pl.ds(pl.multiple_of(n * QB, QB), QB), :]
        stacked = jnp.concatenate([rows[:, h * DH : (h + 1) * DH] for h in range(H)], axis=0)
        key_tiles = [edge_ref[:BLOCK, :], edge_ref[2 * BLOCK : 3 * BLOCK, :]]
        value_tiles = [edge_ref[BLOCK : 2 * BLOCK, :], edge_ref[3 * BLOCK :, :]]
        for i in range(FREE):
            code = codes[i, step * per_step + n]
            source = code // CAP
            row = pl.multiple_of(code % CAP * BLOCK, BLOCK)
            key_tiles.append(table_ref[source, pl.ds(row, BLOCK), :])
            value_tiles.append(table_ref[source, pl.ds(row + CAP * BLOCK, BLOCK), :])
        join = lambda tiles, g: jnp.concatenate(tiles[g * GROUP : (g + 1) * GROUP], axis=0)
        return (
            stacked,
            [join(key_tiles, g) for g in range(groups)],
            [jnp.concatenate([join(value_tiles, g), ones], axis=1) for g in range(groups)],
        )

    def score(block, c, g):
        part = block[0][c * CHUNK : (c + 1) * CHUNK]
        return lax.dot_general(
            part, block[1][g], (((1,), (1,)), ((), ())), preferred_element_type=jnp.float32
        )

    def weigh(block, g, scores, shift):
        weights = jnp.exp2((scores - shift) * SCALE).astype(jnp.bfloat16)
        return jnp.dot(weights, block[2][g], preferred_element_type=jnp.float32)

    def store(n, c, total):
        done = (total[:, :DH] / total[:, DH:]).astype(jnp.bfloat16)
        for i in range(CHUNK // QB):
            h = c * (CHUNK // QB) + i
            row = pl.multiple_of(n * QB, QB)
            out_ref[pl.ds(row, QB), h * DH : (h + 1) * DH] = done[i * QB : (i + 1) * QB]

    largest, total, waiting = None, None, None

    def advance(block, n, c, g, scores, shift):
        nonlocal largest, total
        product = weigh(block, g, scores, shift)
        total = product if g == 0 else total + product
        if g == groups - 1:
            sums = total[:, DH:]
            parts = [sums[i * 8 : (i + 1) * 8] for i in range(CHUNK // 8)]
            largest = functools.reduce(jnp.maximum, parts if largest is None else [largest, *parts])
            store(n, c, total)

    for n in range(per_step):
        block = load(n)
        for c in range(chunks):
            shift = None
            for g in range(groups):
                scores = score(block, c, g)
                if g == 0:
                    shift = jnp.max(scores, axis=1, keepdims=True)
                if waiting is not None:
                    advance(*waiting)
                waiting = (block, n, c, g, scores, shift)
    advance(*waiting)

    @pl.when(jnp.logical_not(jnp.max(largest) < TRUSTED))
    def _():
        @pl.loop(0, per_step)
        def _(n):
            block = load(n)
            for c in range(chunks):
                scores = [score(block, c, g) for g in range(groups)]
                tops = [jnp.max(s, axis=1, keepdims=True) for s in scores]
                top = functools.reduce(jnp.maximum, tops)
                products = [weigh(block, g, scores[g], top) for g in range(groups)]
                store(n, c, functools.reduce(jnp.add, products))


def per_device(queries, keys, values, selected):
    pb_count = lax.axis_size("pb")
    kv_count = lax.axis_size("kv")
    devices = pb_count * kv_count
    blocks_here = keys.shape[0] // BLOCK
    query_blocks = queries.shape[0] // QB

    listed = selected.T
    first = pl.BlockSpec((BLOCK, DH), lambda i: (0, 0))
    last = pl.BlockSpec((BLOCK, DH), lambda i: (blocks_here - 1, 0))
    held = pl.BlockSpec(listed.shape, lambda i: (0, 0))
    message_shape = (devices, 2 * PIECE, DH)
    codes, message = pl.pallas_call(
        functools.partial(prepare, pb_count, kv_count, blocks_here),
        grid=(1,),
        in_specs=[held, first, first, last, last],
        out_specs=[held, pl.BlockSpec(message_shape, lambda i: (0, 0, 0))],
        out_shape=[
            jax.ShapeDtypeStruct(listed.shape, jnp.int32),
            jax.ShapeDtypeStruct(message_shape, jnp.bfloat16),
        ],
    )(listed, keys, values, keys, values)

    held_tiles = pl.pallas_call(
        stage,
        grid=(1,),
        in_specs=[
            pl.BlockSpec(keys.shape, lambda i: (0, 0)),
            pl.BlockSpec(values.shape, lambda i: (0, 0)),
        ],
        out_specs=pl.BlockSpec(memory_space=pltpu.VMEM),
        out_shape=jax.ShapeDtypeStruct((2,) + keys.shape, keys.dtype),
        compiler_params=pltpu.CompilerParams(vmem_limit_bytes=8 << 20),
    )(keys, values)
    answer = exchange(message)
    late = (lax.axis_index(ALL) % PIECES >= PIECES // 2).astype(jnp.int32)
    asked = answer[:, 0, :CAP].astype(jnp.int32).reshape(-1)
    parcel_shape = (devices, 2 * CAP * BLOCK + PIECE, DH)
    parcel_bytes = 2 * math.prod(parcel_shape)
    parcel = pl.pallas_call(
        functools.partial(pack, devices),
        grid_spec=pltpu.PrefetchScalarGridSpec(
            num_scalar_prefetch=2,
            grid=(1,),
            in_specs=[pl.BlockSpec(memory_space=pltpu.VMEM)] * 2,
            out_specs=pl.BlockSpec(memory_space=pltpu.VMEM),
        ),
        out_shape=jax.ShapeDtypeStruct(parcel_shape, keys.dtype),
        compiler_params=pltpu.CompilerParams(vmem_limit_bytes=(8 << 20) + parcel_bytes),
    )(asked, late[None], answer, held_tiles)
    table = exchange(parcel)

    per_step = math.gcd(query_blocks, 12)
    return pl.pallas_call(
        functools.partial(attend, per_step),
        out_shape=jax.ShapeDtypeStruct(queries.shape, queries.dtype),
        grid_spec=pltpu.PrefetchScalarGridSpec(
            num_scalar_prefetch=1,
            grid=(query_blocks // per_step,),
            in_specs=[
                pl.BlockSpec((per_step * QB, H * DH), lambda i, c: (i, 0)),
                pl.BlockSpec(memory_space=pltpu.VMEM),
            ],
            out_specs=pl.BlockSpec((per_step * QB, H * DH), lambda i, c: (i, 0)),
            scratch_shapes=[pltpu.VMEM((4 * BLOCK, DH), jnp.bfloat16)],
        ),
        compiler_params=pltpu.CompilerParams(vmem_limit_bytes=(24 << 20) + parcel_bytes),
    )(codes, queries, table)


def solution(mesh):
    by_query = P(("pb", "kv"), None)
    by_key = P(("kv", "pb"), None)
    return jax.shard_map(
        per_device,
        mesh=mesh,
        in_specs=(by_query, by_key, by_key, by_query),
        out_specs=by_query,
        check_vma=False,
    )
```

```python
import functools
import math

import jax
import jax.numpy as jnp
from jax import lax
from jax.experimental import pallas as pl
from jax.experimental.pallas import tpu as pltpu
from jax.sharding import PartitionSpec as P

H = 8
DH = 128
BLOCK = 64
FREE = 14
QB = 64
CAP = 2
PIECES = 32
PIECE = 2 * BLOCK // PIECES
TILE = 2 * PIECE
CHUNK = 256
GROUP = 4
TRUSTED = 2.0 ** 100
SCALE = DH ** -0.5 * math.log2(math.e)
ALL = ("pb", "kv")


def exchange(array):
    return lax.all_to_all(array, ALL, split_axis=0, concat_axis=0, tiled=True)


def divide(array, n):
    if n & (n - 1) == 0:
        return array >> (n.bit_length() - 1), array & (n - 1)
    return array // n, array % n


def roll_half(tile):
    return jnp.concatenate([tile[PIECE:], tile[:PIECE]], axis=0)


def prepare(pb_count, kv_count, blocks_here, me_ref, selected_ref, fk, fv, lk, lv, code_ref, message_ref):
    devices = pb_count * kv_count
    rows, columns = selected_ref.shape
    owner, locals_ = divide(selected_ref[...], blocks_here)
    owner_kv, owner_pb = divide(owner, pb_count)
    places = owner_pb * kv_count + owner_kv
    ids = lax.broadcasted_iota(jnp.int32, (devices, columns), 0)
    low = jnp.full((devices, columns), blocks_here - 1, jnp.int32)
    high = jnp.zeros((devices, columns), jnp.int32)
    for r in range(rows):
        hit = places[r : r + 1, :] == ids
        local = jnp.broadcast_to(locals_[r : r + 1, :], ids.shape)
        low = jnp.where(hit, jnp.minimum(low, local), low)
        high = jnp.where(hit, jnp.maximum(high, local), high)
    low = jnp.min(low, axis=1, keepdims=True)
    high = jnp.max(high, axis=1, keepdims=True)
    for r in range(rows):
        place, local = places[r : r + 1, :], locals_[r : r + 1, :]
        above = jnp.where((place == ids) & (local > low), 1, 0)
        code_ref[r : r + 1, :] = place * CAP + jnp.max(above, axis=0, keepdims=True)
    lane = lax.broadcasted_iota(jnp.int32, (devices, DH), 1)
    wants = jnp.where(lane == 0, low, jnp.where(lane == 1, high, 0)).astype(jnp.float32)
    first = me_ref[0] == 0
    edge = jnp.concatenate([jnp.where(first, fk[...], lk[...]), jnp.where(first, fv[...], lv[...])], axis=0)
    edge = edge.astype(jnp.float32)
    upper = lax.broadcasted_iota(jnp.int32, (TILE, DH), 0) < PIECE
    for m in range(devices):
        at = m % PIECES // 2 * TILE
        piece = edge[at : at + TILE]
        piece = piece if m % 2 == 0 else roll_half(piece)
        message_ref[m] = jnp.where(upper, piece, wants[m : m + 1]).astype(jnp.bfloat16)


def stage(k_ref, v_ref, held_ref):
    held_ref[0] = k_ref[...]
    held_ref[1] = v_ref[...]


def pack(devices, asked, answer_ref, held_ref, parcel_ref):
    first = answer_ref[0].astype(jnp.float32)
    last = answer_ref[devices - 1].astype(jnp.float32)
    piece = jnp.concatenate([first[:PIECE], last[:PIECE]], axis=0).astype(jnp.bfloat16)

    @pl.loop(0, devices, unroll=4)
    def _(m):
        for slot in range(CAP):
            row = pl.multiple_of(asked[m * CAP + slot] * BLOCK, BLOCK)
            at = slot * BLOCK
            parcel_ref[m, at : at + BLOCK, :] = held_ref[0, pl.ds(row, BLOCK), :]
            at += CAP * BLOCK
            parcel_ref[m, at : at + BLOCK, :] = held_ref[1, pl.ds(row, BLOCK), :]
        parcel_ref[m, 2 * CAP * BLOCK :, :] = piece


def attend(per_step, codes, q_ref, table_ref, out_ref, edge_ref):
    step = pl.program_id(0)

    @pl.when(step == 0)
    def _():
        upper = lax.broadcasted_iota(jnp.int32, (TILE, DH), 0) < PIECE
        firsts, lasts = [], []
        for p in range(0, PIECES, 2):
            even = table_ref[p, 2 * CAP * BLOCK :, :].astype(jnp.float32)
            odd = table_ref[p + 1, 2 * CAP * BLOCK :, :].astype(jnp.float32)
            firsts.append(jnp.where(upper, even, roll_half(odd)))
            lasts.append(jnp.where(upper, roll_half(even), odd))
        edge_ref[...] = jnp.concatenate(firsts + lasts, axis=0).astype(jnp.bfloat16)

    ones = jnp.ones((GROUP * BLOCK, DH), jnp.bfloat16)
    groups = (FREE + 2) // GROUP
    chunks = QB * H // CHUNK

    def load(n):
        rows = q_ref[pl.ds(pl.multiple_of(n * QB, QB), QB), :]
        stacked = jnp.concatenate([rows[:, h * DH : (h + 1) * DH] for h in range(H)], axis=0)
        key_tiles = [edge_ref[:BLOCK, :], edge_ref[2 * BLOCK : 3 * BLOCK, :]]
        value_tiles = [edge_ref[BLOCK : 2 * BLOCK, :], edge_ref[3 * BLOCK :, :]]
        for i in range(FREE):
            code = codes[i, step * per_step + n]
            source = code // CAP
            row = pl.multiple_of(code % CAP * BLOCK, BLOCK)
            key_tiles.append(table_ref[source, pl.ds(row, BLOCK), :])
            value_tiles.append(table_ref[source, pl.ds(row + CAP * BLOCK, BLOCK), :])
        join = lambda tiles, g: jnp.concatenate(tiles[g * GROUP : (g + 1) * GROUP], axis=0)
        return (
            stacked,
            [join(key_tiles, g) for g in range(groups)],
            [jnp.concatenate([join(value_tiles, g), ones], axis=1) for g in range(groups)],
        )

    def score(block, c, g):
        part = block[0][c * CHUNK : (c + 1) * CHUNK]
        return lax.dot_general(
            part, block[1][g], (((1,), (1,)), ((), ())), preferred_element_type=jnp.float32
        )

    def weigh(block, g, scores, shift):
        weights = jnp.exp2((scores - shift) * SCALE).astype(jnp.bfloat16)
        return jnp.dot(weights, block[2][g], preferred_element_type=jnp.float32)

    def store(n, c, total):
        done = (total[:, :DH] / total[:, DH:]).astype(jnp.bfloat16)
        for i in range(CHUNK // QB):
            h = c * (CHUNK // QB) + i
            row = pl.multiple_of(n * QB, QB)
            out_ref[pl.ds(row, QB), h * DH : (h + 1) * DH] = done[i * QB : (i + 1) * QB]

    largest, total, waiting = None, None, None

    def advance(block, n, c, g, scores, shift):
        nonlocal largest, total
        product = weigh(block, g, scores, shift)
        total = product if g == 0 else total + product
        if g == groups - 1:
            sums = total[:, DH:]
            parts = [sums[i * 8 : (i + 1) * 8] for i in range(CHUNK // 8)]
            largest = functools.reduce(jnp.maximum, parts if largest is None else [largest, *parts])
            store(n, c, total)

    for n in range(per_step):
        block = load(n)
        for c in range(chunks):
            shift = None
            for g in range(groups):
                scores = score(block, c, g)
                if g == 0:
                    shift = jnp.max(scores, axis=1, keepdims=True)
                if waiting is not None:
                    advance(*waiting)
                waiting = (block, n, c, g, scores, shift)
    advance(*waiting)

    @pl.when(jnp.logical_not(jnp.max(largest) < TRUSTED))
    def _():
        @pl.loop(0, per_step)
        def _(n):
            block = load(n)
            for c in range(chunks):
                scores = [score(block, c, g) for g in range(groups)]
                tops = [jnp.max(s, axis=1, keepdims=True) for s in scores]
                top = functools.reduce(jnp.maximum, tops)
                products = [weigh(block, g, scores[g], top) for g in range(groups)]
                store(n, c, functools.reduce(jnp.add, products))


def per_device(queries, keys, values, selected):
    pb_count = lax.axis_size("pb")
    kv_count = lax.axis_size("kv")
    devices = pb_count * kv_count
    blocks_here = keys.shape[0] // BLOCK
    query_blocks = queries.shape[0] // QB

    listed = selected.T
    me = lax.axis_index(ALL).astype(jnp.int32)[None]
    first = pl.BlockSpec((BLOCK, DH), lambda i, m: (0, 0))
    last = pl.BlockSpec((BLOCK, DH), lambda i, m: (blocks_here - 1, 0))
    held = pl.BlockSpec(listed.shape, lambda i, m: (0, 0))
    message_shape = (devices, TILE, DH)
    codes, message = pl.pallas_call(
        functools.partial(prepare, pb_count, kv_count, blocks_here),
        grid_spec=pltpu.PrefetchScalarGridSpec(
            num_scalar_prefetch=1,
            grid=(1,),
            in_specs=[held, first, first, last, last],
            out_specs=[held, pl.BlockSpec(message_shape, lambda i, m: (0, 0, 0))],
        ),
        out_shape=[
            jax.ShapeDtypeStruct(listed.shape, jnp.int32),
            jax.ShapeDtypeStruct(message_shape, jnp.bfloat16),
        ],
    )(me, listed, keys, values, keys, values)

    held_tiles = pl.pallas_call(
        stage,
        grid=(1,),
        in_specs=[
            pl.BlockSpec(keys.shape, lambda i: (0, 0)),
            pl.BlockSpec(values.shape, lambda i: (0, 0)),
        ],
        out_specs=pl.BlockSpec(memory_space=pltpu.VMEM),
        out_shape=jax.ShapeDtypeStruct((2,) + keys.shape, keys.dtype),
        compiler_params=pltpu.CompilerParams(vmem_limit_bytes=8 << 20),
    )(keys, values)
    answer = exchange(message)
    asked = answer[:, PIECE, :CAP].astype(jnp.int32).reshape(-1)
    parcel_shape = (devices, 2 * CAP * BLOCK + TILE, DH)
    parcel_bytes = 2 * math.prod(parcel_shape)
    parcel = pl.pallas_call(
        functools.partial(pack, devices),
        grid_spec=pltpu.PrefetchScalarGridSpec(
            num_scalar_prefetch=1,
            grid=(1,),
            in_specs=[pl.BlockSpec(memory_space=pltpu.VMEM)] * 2,
            out_specs=pl.BlockSpec(memory_space=pltpu.VMEM),
        ),
        out_shape=jax.ShapeDtypeStruct(parcel_shape, keys.dtype),
        compiler_params=pltpu.CompilerParams(vmem_limit_bytes=(8 << 20) + parcel_bytes),
    )(asked, answer, held_tiles)
    table = exchange(parcel)

    per_step = math.gcd(query_blocks, 12)
    return pl.pallas_call(
        functools.partial(attend, per_step),
        out_shape=jax.ShapeDtypeStruct(queries.shape, queries.dtype),
        grid_spec=pltpu.PrefetchScalarGridSpec(
            num_scalar_prefetch=1,
            grid=(query_blocks // per_step,),
            in_specs=[
                pl.BlockSpec((per_step * QB, H * DH), lambda i, c: (i, 0)),
                pl.BlockSpec(memory_space=pltpu.VMEM),
            ],
            out_specs=pl.BlockSpec((per_step * QB, H * DH), lambda i, c: (i, 0)),
            scratch_shapes=[pltpu.VMEM((4 * BLOCK, DH), jnp.bfloat16)],
        ),
        compiler_params=pltpu.CompilerParams(vmem_limit_bytes=(24 << 20) + parcel_bytes),
    )(codes, queries, table)


def solution(mesh):
    by_query = P(("pb", "kv"), None)
    by_key = P(("kv", "pb"), None)
    return jax.shard_map(
        per_device,
        mesh=mesh,
        in_specs=(by_query, by_key, by_key, by_query),
        out_specs=by_query,
        check_vma=False,
    )
```

```python
import functools
import math

import jax
import jax.numpy as jnp
from jax import lax
from jax.experimental import pallas as pl
from jax.experimental.pallas import tpu as pltpu
from jax.sharding import PartitionSpec as P

H = 8
DH = 128
BLOCK = 64
FREE = 14
QB = 64
CAP = 2
PIECES = 32
PIECE = 2 * BLOCK // PIECES
TILE = 2 * PIECE
CHUNK = 256
GROUP = 4
TRUSTED = 2.0 ** 100
SCALE = DH ** -0.5 * math.log2(math.e)
ALL = ("pb", "kv")


def exchange(array):
    return lax.all_to_all(array, ALL, split_axis=0, concat_axis=0, tiled=True)


def divide(array, n):
    if n & (n - 1) == 0:
        return array >> (n.bit_length() - 1), array & (n - 1)
    return array // n, array % n


def roll_half(tile):
    return jnp.concatenate([tile[PIECE:], tile[:PIECE]], axis=0)


def wanted(pb_count, kv_count, blocks_here, selected_ref):
    devices = pb_count * kv_count
    rows, columns = selected_ref.shape
    owner, local = divide(selected_ref[...], blocks_here)
    owner_kv, owner_pb = divide(owner, pb_count)
    place = owner_pb * kv_count + owner_kv
    ids = lax.broadcasted_iota(jnp.int32, (devices, columns), 0)
    low = jnp.full((devices, columns), blocks_here - 1, jnp.int32)
    high = jnp.zeros((devices, columns), jnp.int32)
    for r in range(rows):
        hit = place[r : r + 1, :] == ids
        here = jnp.broadcast_to(local[r : r + 1, :], ids.shape)
        low = jnp.where(hit, jnp.minimum(low, here), low)
        high = jnp.where(hit, jnp.maximum(high, here), high)
    low = jnp.min(low, axis=1, keepdims=True)
    high = jnp.max(high, axis=1, keepdims=True)
    return place, local, ids, low, high


def prepare(pb_count, kv_count, blocks_here, me_ref, selected_ref, fk, fv, lk, lv, message_ref):
    devices = pb_count * kv_count
    low, high = wanted(pb_count, kv_count, blocks_here, selected_ref)[3:]
    lane = lax.broadcasted_iota(jnp.int32, (devices, DH), 1)
    wants = jnp.where(lane == 0, low, jnp.where(lane == 1, high, 0)).astype(jnp.float32)
    first = me_ref[0] == 0
    edge = jnp.concatenate([jnp.where(first, fk[...], lk[...]), jnp.where(first, fv[...], lv[...])], axis=0)
    edge = edge.astype(jnp.float32)
    upper = lax.broadcasted_iota(jnp.int32, (TILE, DH), 0) < PIECE
    for m in range(devices):
        at = m % PIECES // 2 * TILE
        piece = edge[at : at + TILE]
        piece = piece if m % 2 == 0 else roll_half(piece)
        message_ref[m] = jnp.where(upper, piece, wants[m : m + 1]).astype(jnp.bfloat16)


def stage(pb_count, kv_count, blocks_here, selected_ref, k_ref, v_ref, held_ref, code_ref):
    held_ref[0] = k_ref[...]
    held_ref[1] = v_ref[...]
    places, locals_, ids, low, _ = wanted(pb_count, kv_count, blocks_here, selected_ref)
    for r in range(selected_ref.shape[0]):
        place, local = places[r : r + 1, :], locals_[r : r + 1, :]
        above = jnp.where((place == ids) & (local > low), 1, 0)
        code_ref[r : r + 1, :] = place * CAP + jnp.max(above, axis=0, keepdims=True)


def pack(devices, asked, answer_ref, held_ref, parcel_ref):
    first = answer_ref[0].astype(jnp.float32)
    last = answer_ref[devices - 1].astype(jnp.float32)
    piece = jnp.concatenate([first[:PIECE], last[:PIECE]], axis=0).astype(jnp.bfloat16)

    @pl.loop(0, devices, unroll=4)
    def _(m):
        for slot in range(CAP):
            row = pl.multiple_of(asked[m * CAP + slot] * BLOCK, BLOCK)
            at = slot * BLOCK
            parcel_ref[m, at : at + BLOCK, :] = held_ref[0, pl.ds(row, BLOCK), :]
            at += CAP * BLOCK
            parcel_ref[m, at : at + BLOCK, :] = held_ref[1, pl.ds(row, BLOCK), :]
        parcel_ref[m, 2 * CAP * BLOCK :, :] = piece


def attend(per_step, codes, q_ref, table_ref, out_ref, edge_ref):
    step = pl.program_id(0)

    @pl.when(step == 0)
    def _():
        upper = lax.broadcasted_iota(jnp.int32, (TILE, DH), 0) < PIECE
        firsts, lasts = [], []
        for p in range(0, PIECES, 2):
            even = table_ref[p, 2 * CAP * BLOCK :, :].astype(jnp.float32)
            odd = table_ref[p + 1, 2 * CAP * BLOCK :, :].astype(jnp.float32)
            firsts.append(jnp.where(upper, even, roll_half(odd)))
            lasts.append(jnp.where(upper, roll_half(even), odd))
        edge_ref[...] = jnp.concatenate(firsts + lasts, axis=0).astype(jnp.bfloat16)

    ones = jnp.ones((GROUP * BLOCK, DH), jnp.bfloat16)
    groups = (FREE + 2) // GROUP
    chunks = QB * H // CHUNK

    def load(n):
        rows = q_ref[pl.ds(pl.multiple_of(n * QB, QB), QB), :]
        stacked = jnp.concatenate([rows[:, h * DH : (h + 1) * DH] for h in range(H)], axis=0)
        key_tiles = [edge_ref[:BLOCK, :], edge_ref[2 * BLOCK : 3 * BLOCK, :]]
        value_tiles = [edge_ref[BLOCK : 2 * BLOCK, :], edge_ref[3 * BLOCK :, :]]
        for i in range(FREE):
            code = codes[i, step * per_step + n]
            source = code // CAP
            row = pl.multiple_of(code % CAP * BLOCK, BLOCK)
            key_tiles.append(table_ref[source, pl.ds(row, BLOCK), :])
            value_tiles.append(table_ref[source, pl.ds(row + CAP * BLOCK, BLOCK), :])
        join = lambda tiles, g: jnp.concatenate(tiles[g * GROUP : (g + 1) * GROUP], axis=0)
        return (
            stacked,
            [join(key_tiles, g) for g in range(groups)],
            [jnp.concatenate([join(value_tiles, g), ones], axis=1) for g in range(groups)],
        )

    def score(block, c, g):
        part = block[0][c * CHUNK : (c + 1) * CHUNK]
        return lax.dot_general(
            part, block[1][g], (((1,), (1,)), ((), ())), preferred_element_type=jnp.float32
        )

    def weigh(block, g, scores, shift):
        weights = jnp.exp2((scores - shift) * SCALE).astype(jnp.bfloat16)
        return jnp.dot(weights, block[2][g], preferred_element_type=jnp.float32)

    def store(n, c, total):
        done = (total[:, :DH] / total[:, DH:]).astype(jnp.bfloat16)
        for i in range(CHUNK // QB):
            h = c * (CHUNK // QB) + i
            row = pl.multiple_of(n * QB, QB)
            out_ref[pl.ds(row, QB), h * DH : (h + 1) * DH] = done[i * QB : (i + 1) * QB]

    largest, total, waiting = None, None, None

    def advance(block, n, c, g, scores, shift):
        nonlocal largest, total
        product = weigh(block, g, scores, shift)
        total = product if g == 0 else total + product
        if g == groups - 1:
            sums = total[:, DH:]
            parts = [sums[i * 8 : (i + 1) * 8] for i in range(CHUNK // 8)]
            largest = functools.reduce(jnp.maximum, parts if largest is None else [largest, *parts])
            store(n, c, total)

    for n in range(per_step):
        block = load(n)
        for c in range(chunks):
            shift = None
            for g in range(groups):
                scores = score(block, c, g)
                if g == 0:
                    shift = jnp.max(scores, axis=1, keepdims=True)
                if waiting is not None:
                    advance(*waiting)
                waiting = (block, n, c, g, scores, shift)
    advance(*waiting)

    @pl.when(jnp.logical_not(jnp.max(largest) < TRUSTED))
    def _():
        @pl.loop(0, per_step)
        def _(n):
            block = load(n)
            for c in range(chunks):
                scores = [score(block, c, g) for g in range(groups)]
                tops = [jnp.max(s, axis=1, keepdims=True) for s in scores]
                top = functools.reduce(jnp.maximum, tops)
                products = [weigh(block, g, scores[g], top) for g in range(groups)]
                store(n, c, functools.reduce(jnp.add, products))


def per_device(queries, keys, values, selected):
    pb_count = lax.axis_size("pb")
    kv_count = lax.axis_size("kv")
    devices = pb_count * kv_count
    blocks_here = keys.shape[0] // BLOCK
    query_blocks = queries.shape[0] // QB

    listed = selected.T
    me = lax.axis_index(ALL).astype(jnp.int32)[None]
    first = pl.BlockSpec((BLOCK, DH), lambda i, m: (0, 0))
    last = pl.BlockSpec((BLOCK, DH), lambda i, m: (blocks_here - 1, 0))
    held = pl.BlockSpec(listed.shape, lambda i, m: (0, 0))
    message_shape = (devices, TILE, DH)
    message = pl.pallas_call(
        functools.partial(prepare, pb_count, kv_count, blocks_here),
        grid_spec=pltpu.PrefetchScalarGridSpec(
            num_scalar_prefetch=1,
            grid=(1,),
            in_specs=[held, first, first, last, last],
            out_specs=pl.BlockSpec(message_shape, lambda i, m: (0, 0, 0)),
        ),
        out_shape=jax.ShapeDtypeStruct(message_shape, jnp.bfloat16),
    )(me, listed, keys, values, keys, values)

    listing = pl.BlockSpec(listed.shape, lambda i: (0, 0))
    held_tiles, codes = pl.pallas_call(
        functools.partial(stage, pb_count, kv_count, blocks_here),
        grid=(1,),
        in_specs=[
            listing,
            pl.BlockSpec(keys.shape, lambda i: (0, 0)),
            pl.BlockSpec(values.shape, lambda i: (0, 0)),
        ],
        out_specs=[pl.BlockSpec(memory_space=pltpu.VMEM), listing],
        out_shape=[
            jax.ShapeDtypeStruct((2,) + keys.shape, keys.dtype),
            jax.ShapeDtypeStruct(listed.shape, jnp.int32),
        ],
        compiler_params=pltpu.CompilerParams(vmem_limit_bytes=8 << 20),
    )(listed, keys, values)
    answer = exchange(message)
    asked = answer[:, PIECE, :CAP].astype(jnp.int32).reshape(-1)
    parcel_shape = (devices, 2 * CAP * BLOCK + TILE, DH)
    parcel_bytes = 2 * math.prod(parcel_shape)
    parcel = pl.pallas_call(
        functools.partial(pack, devices),
        grid_spec=pltpu.PrefetchScalarGridSpec(
            num_scalar_prefetch=1,
            grid=(1,),
            in_specs=[pl.BlockSpec(memory_space=pltpu.VMEM)] * 2,
            out_specs=pl.BlockSpec(memory_space=pltpu.VMEM),
        ),
        out_shape=jax.ShapeDtypeStruct(parcel_shape, keys.dtype),
        compiler_params=pltpu.CompilerParams(vmem_limit_bytes=(8 << 20) + parcel_bytes),
    )(asked, answer, held_tiles)
    table = exchange(parcel)

    per_step = math.gcd(query_blocks, 12)
    return pl.pallas_call(
        functools.partial(attend, per_step),
        out_shape=jax.ShapeDtypeStruct(queries.shape, queries.dtype),
        grid_spec=pltpu.PrefetchScalarGridSpec(
            num_scalar_prefetch=1,
            grid=(query_blocks // per_step,),
            in_specs=[
                pl.BlockSpec((per_step * QB, H * DH), lambda i, c: (i, 0)),
                pl.BlockSpec(memory_space=pltpu.VMEM),
            ],
            out_specs=pl.BlockSpec((per_step * QB, H * DH), lambda i, c: (i, 0)),
            scratch_shapes=[pltpu.VMEM((4 * BLOCK, DH), jnp.bfloat16)],
        ),
        compiler_params=pltpu.CompilerParams(vmem_limit_bytes=(24 << 20) + parcel_bytes),
    )(codes, queries, table)


def solution(mesh):
    by_query = P(("pb", "kv"), None)
    by_key = P(("kv", "pb"), None)
    return jax.shard_map(
        per_device,
        mesh=mesh,
        in_specs=(by_query, by_key, by_key, by_query),
        out_specs=by_query,
        check_vma=False,
    )
```

```python
import functools
import math

import jax
import jax.numpy as jnp
from jax import lax
from jax.experimental import pallas as pl
from jax.experimental.pallas import tpu as pltpu
from jax.sharding import PartitionSpec as P

H = 8
DH = 128
BLOCK = 64
FREE = 14
QB = 64
CAP = 2
PIECES = 32
PIECE = 2 * BLOCK // PIECES
TILE = 2 * PIECE
CHUNK = 256
GROUP = 4
TRUSTED = 2.0 ** 100
SCALE = DH ** -0.5 * math.log2(math.e)
ALL = ("pb", "kv")


def exchange(array):
    return lax.all_to_all(array, ALL, split_axis=0, concat_axis=0, tiled=True)


def divide(array, n):
    if n & (n - 1) == 0:
        return array >> (n.bit_length() - 1), array & (n - 1)
    return array // n, array % n


def roll_half(tile):
    return jnp.concatenate([tile[PIECE:], tile[:PIECE]], axis=0)


def wanted(pb_count, kv_count, blocks_here, selected_ref):
    devices = pb_count * kv_count
    rows, columns = selected_ref.shape
    owner, local = divide(selected_ref[...], blocks_here)
    owner_kv, owner_pb = divide(owner, pb_count)
    place = owner_pb * kv_count + owner_kv
    ids = lax.broadcasted_iota(jnp.int32, (devices, columns), 0)
    low = jnp.full((devices, columns), blocks_here - 1, jnp.int32)
    high = jnp.zeros((devices, columns), jnp.int32)
    for r in range(rows):
        hit = place[r : r + 1, :] == ids
        here = jnp.broadcast_to(local[r : r + 1, :], ids.shape)
        low = jnp.where(hit, jnp.minimum(low, here), low)
        high = jnp.where(hit, jnp.maximum(high, here), high)
    low = jnp.min(low, axis=1, keepdims=True)
    high = jnp.max(high, axis=1, keepdims=True)
    return place, local, ids, low, high


def prepare(pb_count, kv_count, blocks_here, me_ref, selected_ref, edge_k, edge_v, message_ref):
    devices = pb_count * kv_count
    low, high = wanted(pb_count, kv_count, blocks_here, selected_ref)[3:]
    lane = lax.broadcasted_iota(jnp.int32, (devices, DH), 1)
    wants = jnp.where(lane == 0, low, jnp.where(lane == 1, high, 0)).astype(jnp.float32)
    edge = jnp.concatenate([edge_k[...], edge_v[...]], axis=0).astype(jnp.float32)
    upper = lax.broadcasted_iota(jnp.int32, (TILE, DH), 0) < PIECE
    for m in range(devices):
        at = m % PIECES // 2 * TILE
        piece = edge[at : at + TILE]
        piece = piece if m % 2 == 0 else roll_half(piece)
        message_ref[m] = jnp.where(upper, piece, wants[m : m + 1]).astype(jnp.bfloat16)


def stage(pb_count, kv_count, blocks_here, selected_ref, k_ref, v_ref, held_ref, code_ref):
    held_ref[0] = k_ref[...]
    held_ref[1] = v_ref[...]
    places, locals_, ids, low, _ = wanted(pb_count, kv_count, blocks_here, selected_ref)
    for r in range(selected_ref.shape[0]):
        place, local = places[r : r + 1, :], locals_[r : r + 1, :]
        above = jnp.where((place == ids) & (local > low), 1, 0)
        code_ref[r : r + 1, :] = place * CAP + jnp.max(above, axis=0, keepdims=True)


def pack(devices, asked, answer_ref, held_ref, parcel_ref):
    first = answer_ref[0].astype(jnp.float32)
    last = answer_ref[devices - 1].astype(jnp.float32)
    piece = jnp.concatenate([first[:PIECE], last[:PIECE]], axis=0).astype(jnp.bfloat16)

    @pl.loop(0, devices, unroll=8)
    def _(m):
        for slot in range(CAP):
            row = pl.multiple_of(asked[m * CAP + slot] * BLOCK, BLOCK)
            at = slot * BLOCK
            parcel_ref[m, at : at + BLOCK, :] = held_ref[0, pl.ds(row, BLOCK), :]
            at += CAP * BLOCK
            parcel_ref[m, at : at + BLOCK, :] = held_ref[1, pl.ds(row, BLOCK), :]
        parcel_ref[m, 2 * CAP * BLOCK :, :] = piece


def attend(per_step, codes, q_ref, table_ref, out_ref, edge_ref):
    step = pl.program_id(0)

    @pl.when(step == 0)
    def _():
        upper = lax.broadcasted_iota(jnp.int32, (TILE, DH), 0) < PIECE
        firsts, lasts = [], []
        for p in range(0, PIECES, 2):
            even = table_ref[p, 2 * CAP * BLOCK :, :].astype(jnp.float32)
            odd = table_ref[p + 1, 2 * CAP * BLOCK :, :].astype(jnp.float32)
            firsts.append(jnp.where(upper, even, roll_half(odd)))
            lasts.append(jnp.where(upper, roll_half(even), odd))
        edge_ref[...] = jnp.concatenate(firsts + lasts, axis=0).astype(jnp.bfloat16)

    ones = jnp.ones((GROUP * BLOCK, DH), jnp.bfloat16)
    groups = (FREE + 2) // GROUP
    chunks = QB * H // CHUNK

    def load(n):
        rows = q_ref[pl.ds(pl.multiple_of(n * QB, QB), QB), :]
        stacked = jnp.concatenate([rows[:, h * DH : (h + 1) * DH] for h in range(H)], axis=0)
        key_tiles = [edge_ref[:BLOCK, :], edge_ref[2 * BLOCK : 3 * BLOCK, :]]
        value_tiles = [edge_ref[BLOCK : 2 * BLOCK, :], edge_ref[3 * BLOCK :, :]]
        for i in range(FREE):
            code = codes[i, step * per_step + n]
            source = code // CAP
            row = pl.multiple_of(code % CAP * BLOCK, BLOCK)
            key_tiles.append(table_ref[source, pl.ds(row, BLOCK), :])
            value_tiles.append(table_ref[source, pl.ds(row + CAP * BLOCK, BLOCK), :])
        join = lambda tiles, g: jnp.concatenate(tiles[g * GROUP : (g + 1) * GROUP], axis=0)
        return (
            stacked,
            [join(key_tiles, g) for g in range(groups)],
            [jnp.concatenate([join(value_tiles, g), ones], axis=1) for g in range(groups)],
        )

    def score(block, c, g):
        part = block[0][c * CHUNK : (c + 1) * CHUNK]
        return lax.dot_general(
            part, block[1][g], (((1,), (1,)), ((), ())), preferred_element_type=jnp.float32
        )

    def weigh(block, g, scores, shift):
        weights = jnp.exp2((scores - shift) * SCALE).astype(jnp.bfloat16)
        return jnp.dot(weights, block[2][g], preferred_element_type=jnp.float32)

    def store(n, c, total):
        done = (total[:, :DH] / total[:, DH:]).astype(jnp.bfloat16)
        for i in range(CHUNK // QB):
            h = c * (CHUNK // QB) + i
            row = pl.multiple_of(n * QB, QB)
            out_ref[pl.ds(row, QB), h * DH : (h + 1) * DH] = done[i * QB : (i + 1) * QB]

    largest, total, waiting = None, None, None

    def advance(block, n, c, g, scores, shift):
        nonlocal largest, total
        product = weigh(block, g, scores, shift)
        total = product if g == 0 else total + product
        if g == groups - 1:
            sums = total[:, DH:]
            parts = [sums[i * 32 : (i + 1) * 32] for i in range(CHUNK // 32)]
            largest = functools.reduce(jnp.maximum, parts if largest is None else [largest, *parts])
            store(n, c, total)

    for n in range(per_step):
        block = load(n)
        for c in range(chunks):
            shift = None
            for g in range(groups):
                scores = score(block, c, g)
                if g == 0:
                    shift = jnp.max(scores, axis=1, keepdims=True)
                if waiting is not None:
                    advance(*waiting)
                waiting = (block, n, c, g, scores, shift)
    advance(*waiting)

    @pl.when(jnp.logical_not(jnp.max(largest) < TRUSTED))
    def _():
        @pl.loop(0, per_step)
        def _(n):
            block = load(n)
            for c in range(chunks):
                scores = [score(block, c, g) for g in range(groups)]
                tops = [jnp.max(s, axis=1, keepdims=True) for s in scores]
                top = functools.reduce(jnp.maximum, tops)
                products = [weigh(block, g, scores[g], top) for g in range(groups)]
                store(n, c, functools.reduce(jnp.add, products))


def per_device(queries, keys, values, selected):
    pb_count = lax.axis_size("pb")
    kv_count = lax.axis_size("kv")
    devices = pb_count * kv_count
    blocks_here = keys.shape[0] // BLOCK
    query_blocks = queries.shape[0] // QB

    listed = selected.T
    me = lax.axis_index(ALL).astype(jnp.int32)[None]
    edge = pl.BlockSpec((BLOCK, DH), lambda i, m: (jnp.where(m[0] == 0, 0, blocks_here - 1), 0))
    held = pl.BlockSpec(listed.shape, lambda i, m: (0, 0))
    message_shape = (devices, TILE, DH)
    message = pl.pallas_call(
        functools.partial(prepare, pb_count, kv_count, blocks_here),
        grid_spec=pltpu.PrefetchScalarGridSpec(
            num_scalar_prefetch=1,
            grid=(1,),
            in_specs=[held, edge, edge],
            out_specs=pl.BlockSpec(message_shape, lambda i, m: (0, 0, 0)),
        ),
        out_shape=jax.ShapeDtypeStruct(message_shape, jnp.bfloat16),
    )(me, listed, keys, values)

    listing = pl.BlockSpec(listed.shape, lambda i: (0, 0))
    held_tiles, codes = pl.pallas_call(
        functools.partial(stage, pb_count, kv_count, blocks_here),
        grid=(1,),
        in_specs=[
            listing,
            pl.BlockSpec(keys.shape, lambda i: (0, 0)),
            pl.BlockSpec(values.shape, lambda i: (0, 0)),
        ],
        out_specs=[pl.BlockSpec(memory_space=pltpu.VMEM), listing],
        out_shape=[
            jax.ShapeDtypeStruct((2,) + keys.shape, keys.dtype),
            jax.ShapeDtypeStruct(listed.shape, jnp.int32),
        ],
        compiler_params=pltpu.CompilerParams(vmem_limit_bytes=8 << 20),
    )(listed, keys, values)
    answer = exchange(message)
    asked = answer[:, PIECE, :CAP].astype(jnp.int32).reshape(-1)
    parcel_shape = (devices, 2 * CAP * BLOCK + TILE, DH)
    parcel_bytes = 2 * math.prod(parcel_shape)
    parcel = pl.pallas_call(
        functools.partial(pack, devices),
        grid_spec=pltpu.PrefetchScalarGridSpec(
            num_scalar_prefetch=1,
            grid=(1,),
            in_specs=[pl.BlockSpec(memory_space=pltpu.VMEM)] * 2,
            out_specs=pl.BlockSpec(memory_space=pltpu.VMEM),
        ),
        out_shape=jax.ShapeDtypeStruct(parcel_shape, keys.dtype),
        compiler_params=pltpu.CompilerParams(vmem_limit_bytes=(8 << 20) + parcel_bytes),
    )(asked, answer, held_tiles)
    table = exchange(parcel)

    per_step = math.gcd(query_blocks, 12)
    return pl.pallas_call(
        functools.partial(attend, per_step),
        out_shape=jax.ShapeDtypeStruct(queries.shape, queries.dtype),
        grid_spec=pltpu.PrefetchScalarGridSpec(
            num_scalar_prefetch=1,
            grid=(query_blocks // per_step,),
            in_specs=[
                pl.BlockSpec((per_step * QB, H * DH), lambda i, c: (i, 0)),
                pl.BlockSpec(memory_space=pltpu.VMEM),
            ],
            out_specs=pl.BlockSpec((per_step * QB, H * DH), lambda i, c: (i, 0)),
            scratch_shapes=[pltpu.VMEM((4 * BLOCK, DH), jnp.bfloat16)],
        ),
        compiler_params=pltpu.CompilerParams(vmem_limit_bytes=(24 << 20) + parcel_bytes),
    )(codes, queries, table)


def solution(mesh):
    by_query = P(("pb", "kv"), None)
    by_key = P(("kv", "pb"), None)
    return jax.shard_map(
        per_device,
        mesh=mesh,
        in_specs=(by_query, by_key, by_key, by_query),
        out_specs=by_query,
        check_vma=False,
    )
```

```python
import functools
import math

import jax
import jax.numpy as jnp
from jax import lax
from jax.experimental import pallas as pl
from jax.experimental.pallas import tpu as pltpu
from jax.sharding import PartitionSpec as P

H = 8
DH = 128
BLOCK = 64
FREE = 14
QB = 64
CAP = 2
PIECES = 32
PIECE = 2 * BLOCK // PIECES
TILE = 2 * PIECE
CHUNK = 256
GROUP = 8
TRUSTED = 2.0 ** 100
SCALE = DH ** -0.5 * math.log2(math.e)
ALL = ("pb", "kv")


def exchange(array):
    return lax.all_to_all(array, ALL, split_axis=0, concat_axis=0, tiled=True)


def divide(array, n):
    if n & (n - 1) == 0:
        return array >> (n.bit_length() - 1), array & (n - 1)
    return array // n, array % n


def roll_half(tile):
    return jnp.concatenate([tile[PIECE:], tile[:PIECE]], axis=0)


def wanted(pb_count, kv_count, blocks_here, selected_ref):
    devices = pb_count * kv_count
    rows, columns = selected_ref.shape
    owner, local = divide(selected_ref[...], blocks_here)
    owner_kv, owner_pb = divide(owner, pb_count)
    place = owner_pb * kv_count + owner_kv
    ids = lax.broadcasted_iota(jnp.int32, (devices, columns), 0)
    low = jnp.full((devices, columns), blocks_here - 1, jnp.int32)
    high = jnp.zeros((devices, columns), jnp.int32)
    for r in range(rows):
        hit = place[r : r + 1, :] == ids
        here = jnp.broadcast_to(local[r : r + 1, :], ids.shape)
        low = jnp.where(hit, jnp.minimum(low, here), low)
        high = jnp.where(hit, jnp.maximum(high, here), high)
    low = jnp.min(low, axis=1, keepdims=True)
    high = jnp.max(high, axis=1, keepdims=True)
    return place, local, ids, low, high


def prepare(pb_count, kv_count, blocks_here, me_ref, selected_ref, edge_k, edge_v, message_ref):
    devices = pb_count * kv_count
    low, high = wanted(pb_count, kv_count, blocks_here, selected_ref)[3:]
    lane = lax.broadcasted_iota(jnp.int32, (devices, DH), 1)
    wants = jnp.where(lane == 0, low, jnp.where(lane == 1, high, 0)).astype(jnp.float32)
    edge = jnp.concatenate([edge_k[...], edge_v[...]], axis=0).astype(jnp.float32)
    upper = lax.broadcasted_iota(jnp.int32, (TILE, DH), 0) < PIECE
    for m in range(devices):
        at = m % PIECES // 2 * TILE
        piece = edge[at : at + TILE]
        piece = piece if m % 2 == 0 else roll_half(piece)
        message_ref[m] = jnp.where(upper, piece, wants[m : m + 1]).astype(jnp.bfloat16)


def stage(pb_count, kv_count, blocks_here, selected_ref, k_ref, v_ref, held_ref, code_ref):
    held_ref[0] = k_ref[...]
    held_ref[1] = v_ref[...]
    places, locals_, ids, low, _ = wanted(pb_count, kv_count, blocks_here, selected_ref)
    for r in range(selected_ref.shape[0]):
        place, local = places[r : r + 1, :], locals_[r : r + 1, :]
        above = jnp.where((place == ids) & (local > low), 1, 0)
        code_ref[r : r + 1, :] = place * CAP + jnp.max(above, axis=0, keepdims=True)


def pack(devices, asked, answer_ref, held_ref, parcel_ref):
    first = answer_ref[0].astype(jnp.float32)
    last = answer_ref[devices - 1].astype(jnp.float32)
    piece = jnp.concatenate([first[:PIECE], last[:PIECE]], axis=0).astype(jnp.bfloat16)

    @pl.loop(0, devices, unroll=8)
    def _(m):
        for slot in range(CAP):
            row = pl.multiple_of(asked[m * CAP + slot] * BLOCK, BLOCK)
            at = slot * BLOCK
            parcel_ref[m, at : at + BLOCK, :] = held_ref[0, pl.ds(row, BLOCK), :]
            at += CAP * BLOCK
            parcel_ref[m, at : at + BLOCK, :] = held_ref[1, pl.ds(row, BLOCK), :]
        parcel_ref[m, 2 * CAP * BLOCK :, :] = piece


def attend(per_step, codes, q_ref, table_ref, out_ref, edge_ref):
    step = pl.program_id(0)

    @pl.when(step == 0)
    def _():
        upper = lax.broadcasted_iota(jnp.int32, (TILE, DH), 0) < PIECE
        firsts, lasts = [], []
        for p in range(0, PIECES, 2):
            even = table_ref[p, 2 * CAP * BLOCK :, :].astype(jnp.float32)
            odd = table_ref[p + 1, 2 * CAP * BLOCK :, :].astype(jnp.float32)
            firsts.append(jnp.where(upper, even, roll_half(odd)))
            lasts.append(jnp.where(upper, roll_half(even), odd))
        edge_ref[...] = jnp.concatenate(firsts + lasts, axis=0).astype(jnp.bfloat16)

    ones = jnp.ones((GROUP * BLOCK, DH), jnp.bfloat16)
    groups = (FREE + 2) // GROUP
    chunks = QB * H // CHUNK

    def load(n):
        rows = q_ref[pl.ds(pl.multiple_of(n * QB, QB), QB), :]
        stacked = jnp.concatenate([rows[:, h * DH : (h + 1) * DH] for h in range(H)], axis=0)
        key_tiles = [edge_ref[:BLOCK, :], edge_ref[2 * BLOCK : 3 * BLOCK, :]]
        value_tiles = [edge_ref[BLOCK : 2 * BLOCK, :], edge_ref[3 * BLOCK :, :]]
        for i in range(FREE):
            code = codes[i, step * per_step + n]
            source = code // CAP
            row = pl.multiple_of(code % CAP * BLOCK, BLOCK)
            key_tiles.append(table_ref[source, pl.ds(row, BLOCK), :])
            value_tiles.append(table_ref[source, pl.ds(row + CAP * BLOCK, BLOCK), :])
        join = lambda tiles, g: jnp.concatenate(tiles[g * GROUP : (g + 1) * GROUP], axis=0)
        return (
            stacked,
            [join(key_tiles, g) for g in range(groups)],
            [jnp.concatenate([join(value_tiles, g), ones], axis=1) for g in range(groups)],
        )

    def score(block, c, g):
        part = block[0][c * CHUNK : (c + 1) * CHUNK]
        return lax.dot_general(
            part, block[1][g], (((1,), (1,)), ((), ())), preferred_element_type=jnp.float32
        )

    def weigh(block, g, scores, shift):
        weights = jnp.exp2((scores - shift) * SCALE).astype(jnp.bfloat16)
        return jnp.dot(weights, block[2][g], preferred_element_type=jnp.float32)

    def store(n, c, total):
        done = (total[:, :DH] / total[:, DH:]).astype(jnp.bfloat16)
        for i in range(CHUNK // QB):
            h = c * (CHUNK // QB) + i
            row = pl.multiple_of(n * QB, QB)
            out_ref[pl.ds(row, QB), h * DH : (h + 1) * DH] = done[i * QB : (i + 1) * QB]

    largest, total, waiting = None, None, None

    def advance(block, n, c, g, scores, shift):
        nonlocal largest, total
        product = weigh(block, g, scores, shift)
        total = product if g == 0 else total + product
        if g == groups - 1:
            sums = total[:, DH:]
            parts = [sums[i * 32 : (i + 1) * 32] for i in range(CHUNK // 32)]
            largest = functools.reduce(jnp.maximum, parts if largest is None else [largest, *parts])
            store(n, c, total)

    for n in range(per_step):
        block = load(n)
        for c in range(chunks):
            shift = None
            for g in range(groups):
                scores = score(block, c, g)
                if g == 0:
                    shift = jnp.max(scores, axis=1, keepdims=True)
                if waiting is not None:
                    advance(*waiting)
                waiting = (block, n, c, g, scores, shift)
    advance(*waiting)

    @pl.when(jnp.logical_not(jnp.max(largest) < TRUSTED))
    def _():
        @pl.loop(0, per_step)
        def _(n):
            block = load(n)
            for c in range(chunks):
                scores = [score(block, c, g) for g in range(groups)]
                tops = [jnp.max(s, axis=1, keepdims=True) for s in scores]
                top = functools.reduce(jnp.maximum, tops)
                products = [weigh(block, g, scores[g], top) for g in range(groups)]
                store(n, c, functools.reduce(jnp.add, products))


def per_device(queries, keys, values, selected):
    pb_count = lax.axis_size("pb")
    kv_count = lax.axis_size("kv")
    devices = pb_count * kv_count
    blocks_here = keys.shape[0] // BLOCK
    query_blocks = queries.shape[0] // QB

    listed = selected.T
    me = lax.axis_index(ALL).astype(jnp.int32)[None]
    edge = pl.BlockSpec((BLOCK, DH), lambda i, m: (jnp.where(m[0] == 0, 0, blocks_here - 1), 0))
    held = pl.BlockSpec(listed.shape, lambda i, m: (0, 0))
    message_shape = (devices, TILE, DH)
    message = pl.pallas_call(
        functools.partial(prepare, pb_count, kv_count, blocks_here),
        grid_spec=pltpu.PrefetchScalarGridSpec(
            num_scalar_prefetch=1,
            grid=(1,),
            in_specs=[held, edge, edge],
            out_specs=pl.BlockSpec(message_shape, lambda i, m: (0, 0, 0)),
        ),
        out_shape=jax.ShapeDtypeStruct(message_shape, jnp.bfloat16),
    )(me, listed, keys, values)

    listing = pl.BlockSpec(listed.shape, lambda i: (0, 0))
    held_tiles, codes = pl.pallas_call(
        functools.partial(stage, pb_count, kv_count, blocks_here),
        grid=(1,),
        in_specs=[
            listing,
            pl.BlockSpec(keys.shape, lambda i: (0, 0)),
            pl.BlockSpec(values.shape, lambda i: (0, 0)),
        ],
        out_specs=[pl.BlockSpec(memory_space=pltpu.VMEM), listing],
        out_shape=[
            jax.ShapeDtypeStruct((2,) + keys.shape, keys.dtype),
            jax.ShapeDtypeStruct(listed.shape, jnp.int32),
        ],
        compiler_params=pltpu.CompilerParams(vmem_limit_bytes=8 << 20),
    )(listed, keys, values)
    answer = exchange(message)
    asked = answer[:, PIECE, :CAP].astype(jnp.int32).reshape(-1)
    parcel_shape = (devices, 2 * CAP * BLOCK + TILE, DH)
    parcel_bytes = 2 * math.prod(parcel_shape)
    parcel = pl.pallas_call(
        functools.partial(pack, devices),
        grid_spec=pltpu.PrefetchScalarGridSpec(
            num_scalar_prefetch=1,
            grid=(1,),
            in_specs=[pl.BlockSpec(memory_space=pltpu.VMEM)] * 2,
            out_specs=pl.BlockSpec(memory_space=pltpu.VMEM),
        ),
        out_shape=jax.ShapeDtypeStruct(parcel_shape, keys.dtype),
        compiler_params=pltpu.CompilerParams(vmem_limit_bytes=(8 << 20) + parcel_bytes),
    )(asked, answer, held_tiles)
    table = exchange(parcel)

    per_step = math.gcd(query_blocks, 12)
    return pl.pallas_call(
        functools.partial(attend, per_step),
        out_shape=jax.ShapeDtypeStruct(queries.shape, queries.dtype),
        grid_spec=pltpu.PrefetchScalarGridSpec(
            num_scalar_prefetch=1,
            grid=(query_blocks // per_step,),
            in_specs=[
                pl.BlockSpec((per_step * QB, H * DH), lambda i, c: (i, 0)),
                pl.BlockSpec(memory_space=pltpu.VMEM),
            ],
            out_specs=pl.BlockSpec((per_step * QB, H * DH), lambda i, c: (i, 0)),
            scratch_shapes=[pltpu.VMEM((4 * BLOCK, DH), jnp.bfloat16)],
        ),
        compiler_params=pltpu.CompilerParams(vmem_limit_bytes=(24 << 20) + parcel_bytes),
    )(codes, queries, table)


def solution(mesh):
    by_query = P(("pb", "kv"), None)
    by_key = P(("kv", "pb"), None)
    return jax.shard_map(
        per_device,
        mesh=mesh,
        in_specs=(by_query, by_key, by_key, by_query),
        out_specs=by_query,
        check_vma=False,
    )
```

```python
import functools
import math

import jax
import jax.numpy as jnp
from jax import lax
from jax.experimental import pallas as pl
from jax.experimental.pallas import tpu as pltpu
from jax.sharding import PartitionSpec as P

H = 8
DH = 128
BLOCK = 64
FREE = 14
QB = 64
CAP = 2
PIECES = 32
PIECE = 2 * BLOCK // PIECES
TILE = 2 * PIECE
CHUNK = 256
GROUP = 4
TRUSTED = 2.0 ** 100
SCALE = DH ** -0.5 * math.log2(math.e)
ALL = ("pb", "kv")


def exchange(array):
    return lax.all_to_all(array, ALL, split_axis=0, concat_axis=0, tiled=True)


def divide(array, n):
    if n & (n - 1) == 0:
        return array >> (n.bit_length() - 1), array & (n - 1)
    return array // n, array % n


def roll_half(tile):
    return jnp.concatenate([tile[PIECE:], tile[:PIECE]], axis=0)


def wanted(pb_count, kv_count, blocks_here, selected_ref):
    devices = pb_count * kv_count
    rows, columns = selected_ref.shape
    owner, local = divide(selected_ref[...], blocks_here)
    owner_kv, owner_pb = divide(owner, pb_count)
    place = owner_pb * kv_count + owner_kv
    ids = lax.broadcasted_iota(jnp.int32, (devices, columns), 0)
    low = jnp.full((devices, columns), blocks_here - 1, jnp.int32)
    high = jnp.zeros((devices, columns), jnp.int32)
    for r in range(rows):
        hit = place[r : r + 1, :] == ids
        here = jnp.broadcast_to(local[r : r + 1, :], ids.shape)
        low = jnp.where(hit, jnp.minimum(low, here), low)
        high = jnp.where(hit, jnp.maximum(high, here), high)
    low = jnp.min(low, axis=1, keepdims=True)
    high = jnp.max(high, axis=1, keepdims=True)
    return place, local, ids, low, high


def prepare(pb_count, kv_count, blocks_here, me_ref, selected_ref, edge_k, edge_v, message_ref):
    devices = pb_count * kv_count
    low, high = wanted(pb_count, kv_count, blocks_here, selected_ref)[3:]
    lane = lax.broadcasted_iota(jnp.int32, (devices, DH), 1)
    wants = jnp.where(lane == 0, low, jnp.where(lane == 1, high, 0)).astype(jnp.float32)
    edge = jnp.concatenate([edge_k[...], edge_v[...]], axis=0).astype(jnp.float32)
    upper = lax.broadcasted_iota(jnp.int32, (TILE, DH), 0) < PIECE
    for m in range(devices):
        at = m % PIECES // 2 * TILE
        piece = edge[at : at + TILE]
        piece = piece if m % 2 == 0 else roll_half(piece)
        message_ref[m] = jnp.where(upper, piece, wants[m : m + 1]).astype(jnp.bfloat16)


def stage(pb_count, kv_count, blocks_here, selected_ref, k_ref, v_ref, held_ref, code_ref):
    held_ref[0] = k_ref[...]
    held_ref[1] = v_ref[...]
    places, locals_, ids, low, _ = wanted(pb_count, kv_count, blocks_here, selected_ref)
    for r in range(selected_ref.shape[0]):
        place, local = places[r : r + 1, :], locals_[r : r + 1, :]
        above = jnp.where((place == ids) & (local > low), 1, 0)
        code_ref[r : r + 1, :] = place * CAP + jnp.max(above, axis=0, keepdims=True)


def pack(devices, asked, answer_ref, held_ref, parcel_ref):
    first = answer_ref[0].astype(jnp.float32)
    last = answer_ref[devices - 1].astype(jnp.float32)
    piece = jnp.concatenate([first[:PIECE], last[:PIECE]], axis=0).astype(jnp.bfloat16)

    @pl.loop(0, devices, unroll=8)
    def _(m):
        for slot in range(CAP):
            row = pl.multiple_of(asked[m * CAP + slot] * BLOCK, BLOCK)
            at = slot * BLOCK
            parcel_ref[m, at : at + BLOCK, :] = held_ref[0, pl.ds(row, BLOCK), :]
            at += CAP * BLOCK
            parcel_ref[m, at : at + BLOCK, :] = held_ref[1, pl.ds(row, BLOCK), :]
        parcel_ref[m, 2 * CAP * BLOCK :, :] = piece


def attend(per_step, codes, q_ref, table_ref, out_ref, edge_ref):
    step = pl.program_id(0)

    @pl.when(step == 0)
    def _():
        upper = lax.broadcasted_iota(jnp.int32, (TILE, DH), 0) < PIECE
        firsts, lasts = [], []
        for p in range(0, PIECES, 2):
            even = table_ref[p, 2 * CAP * BLOCK :, :].astype(jnp.float32)
            odd = table_ref[p + 1, 2 * CAP * BLOCK :, :].astype(jnp.float32)
            firsts.append(jnp.where(upper, even, roll_half(odd)))
            lasts.append(jnp.where(upper, roll_half(even), odd))
        edge_ref[...] = jnp.concatenate(firsts + lasts, axis=0).astype(jnp.bfloat16)

    ones = jnp.ones((GROUP * BLOCK, DH), jnp.bfloat16)
    groups = (FREE + 2) // GROUP
    chunks = QB * H // CHUNK

    def load(n):
        rows = q_ref[pl.ds(pl.multiple_of(n * QB, QB), QB), :]
        stacked = jnp.concatenate([rows[:, h * DH : (h + 1) * DH] for h in range(H)], axis=0)
        key_tiles = [edge_ref[:BLOCK, :], edge_ref[2 * BLOCK : 3 * BLOCK, :]]
        value_tiles = [edge_ref[BLOCK : 2 * BLOCK, :], edge_ref[3 * BLOCK :, :]]
        for i in range(FREE):
            code = codes[i, step * per_step + n]
            source = code // CAP
            row = pl.multiple_of(code % CAP * BLOCK, BLOCK)
            key_tiles.append(table_ref[source, pl.ds(row, BLOCK), :])
            value_tiles.append(table_ref[source, pl.ds(row + CAP * BLOCK, BLOCK), :])
        join = lambda tiles, g: jnp.concatenate(tiles[g * GROUP : (g + 1) * GROUP], axis=0)
        return (
            stacked,
            [join(key_tiles, g) for g in range(groups)],
            [jnp.concatenate([join(value_tiles, g), ones], axis=1) for g in range(groups)],
        )

    def score(block, c, g):
        part = block[0][c * CHUNK : (c + 1) * CHUNK]
        return lax.dot_general(
            part, block[1][g], (((1,), (1,)), ((), ())), preferred_element_type=jnp.float32
        )

    def weigh(block, g, scores, shift):
        weights = jnp.exp2((scores - shift) * SCALE).astype(jnp.bfloat16)
        return jnp.dot(weights, block[2][g], preferred_element_type=jnp.float32)

    def store(n, c, total):
        done = (total[:, :DH] / total[:, DH:]).astype(jnp.bfloat16)
        for i in range(CHUNK // QB):
            h = c * (CHUNK // QB) + i
            row = pl.multiple_of(n * QB, QB)
            out_ref[pl.ds(row, QB), h * DH : (h + 1) * DH] = done[i * QB : (i + 1) * QB]

    largest, total, waiting = None, None, None

    def advance(block, n, c, g, scores, shift):
        nonlocal largest, total
        product = weigh(block, g, scores, shift)
        total = product if g == 0 else total + product
        if g == groups - 1:
            sums = total[:, DH:]
            parts = [sums[i * 32 : (i + 1) * 32] for i in range(CHUNK // 32)]
            largest = functools.reduce(jnp.maximum, parts if largest is None else [largest, *parts])
            store(n, c, total)

    for n in range(per_step):
        block = load(n)
        for c in range(chunks):
            shift = None
            for g in range(groups):
                scores = score(block, c, g)
                if g == 0:
                    shift = jnp.max(scores, axis=1, keepdims=True)
                if waiting is not None:
                    advance(*waiting)
                waiting = (block, n, c, g, scores, shift)
    advance(*waiting)

    @pl.when(jnp.logical_not(jnp.max(largest) < TRUSTED))
    def _():
        @pl.loop(0, per_step)
        def _(n):
            block = load(n)
            for c in range(chunks):
                scores = [score(block, c, g) for g in range(groups)]
                tops = [jnp.max(s, axis=1, keepdims=True) for s in scores]
                top = functools.reduce(jnp.maximum, tops)
                products = [weigh(block, g, scores[g], top) for g in range(groups)]
                store(n, c, functools.reduce(jnp.add, products))


def per_device(queries, keys, values, selected):
    pb_count = lax.axis_size("pb")
    kv_count = lax.axis_size("kv")
    devices = pb_count * kv_count
    blocks_here = keys.shape[0] // BLOCK
    query_blocks = queries.shape[0] // QB

    listed = selected.T
    me = lax.axis_index(ALL).astype(jnp.int32)[None]
    edge = pl.BlockSpec((BLOCK, DH), lambda i, m: (jnp.where(m[0] == 0, 0, blocks_here - 1), 0))
    held = pl.BlockSpec(listed.shape, lambda i, m: (0, 0))
    message_shape = (devices, TILE, DH)
    message = pl.pallas_call(
        functools.partial(prepare, pb_count, kv_count, blocks_here),
        grid_spec=pltpu.PrefetchScalarGridSpec(
            num_scalar_prefetch=1,
            grid=(1,),
            in_specs=[held, edge, edge],
            out_specs=pl.BlockSpec(memory_space=pltpu.VMEM),
        ),
        out_shape=jax.ShapeDtypeStruct(message_shape, jnp.bfloat16),
    )(me, listed, keys, values)

    listing = pl.BlockSpec(listed.shape, lambda i: (0, 0))
    held_tiles, codes = pl.pallas_call(
        functools.partial(stage, pb_count, kv_count, blocks_here),
        grid=(1,),
        in_specs=[
            listing,
            pl.BlockSpec(keys.shape, lambda i: (0, 0)),
            pl.BlockSpec(values.shape, lambda i: (0, 0)),
        ],
        out_specs=[pl.BlockSpec(memory_space=pltpu.VMEM), listing],
        out_shape=[
            jax.ShapeDtypeStruct((2,) + keys.shape, keys.dtype),
            jax.ShapeDtypeStruct(listed.shape, jnp.int32),
        ],
        compiler_params=pltpu.CompilerParams(vmem_limit_bytes=8 << 20),
    )(listed, keys, values)
    answer = exchange(message)
    asked = answer[:, PIECE, :CAP].astype(jnp.int32).reshape(-1)
    parcel_shape = (devices, 2 * CAP * BLOCK + TILE, DH)
    parcel_bytes = 2 * math.prod(parcel_shape)
    parcel = pl.pallas_call(
        functools.partial(pack, devices),
        grid_spec=pltpu.PrefetchScalarGridSpec(
            num_scalar_prefetch=1,
            grid=(1,),
            in_specs=[pl.BlockSpec(memory_space=pltpu.VMEM)] * 2,
            out_specs=pl.BlockSpec(memory_space=pltpu.VMEM),
        ),
        out_shape=jax.ShapeDtypeStruct(parcel_shape, keys.dtype),
        compiler_params=pltpu.CompilerParams(vmem_limit_bytes=(8 << 20) + parcel_bytes),
    )(asked, answer, held_tiles)
    table = exchange(parcel)

    per_step = math.gcd(query_blocks, 12)
    return pl.pallas_call(
        functools.partial(attend, per_step),
        out_shape=jax.ShapeDtypeStruct(queries.shape, queries.dtype),
        grid_spec=pltpu.PrefetchScalarGridSpec(
            num_scalar_prefetch=1,
            grid=(query_blocks // per_step,),
            in_specs=[
                pl.BlockSpec((per_step * QB, H * DH), lambda i, c: (i, 0)),
                pl.BlockSpec(memory_space=pltpu.VMEM),
            ],
            out_specs=pl.BlockSpec((per_step * QB, H * DH), lambda i, c: (i, 0)),
            scratch_shapes=[pltpu.VMEM((4 * BLOCK, DH), jnp.bfloat16)],
        ),
        compiler_params=pltpu.CompilerParams(vmem_limit_bytes=(24 << 20) + parcel_bytes),
    )(codes, queries, table)


def solution(mesh):
    by_query = P(("pb", "kv"), None)
    by_key = P(("kv", "pb"), None)
    return jax.shard_map(
        per_device,
        mesh=mesh,
        in_specs=(by_query, by_key, by_key, by_query),
        out_specs=by_query,
        check_vma=False,
    )
```
